512 devices in a mesh: row: 32 (over y, x), col: 16 (over z, core).
Axes of the slice: x: 4, y: 8, z: 8, core: 2. Of those that a mesh axis runs over, the one named last changes fastest.
Arguments:
- tokens: bfloat16 [6144, 8192], P('row', 'col'), may hold values from -6 to 6
- weight_blocks: bfloat16 [32, 16, 4, 128, 128], P('row', 'col'), may hold values from -0.1875 to 0.1875
- block_slots: int32 [32, 16, 4], P('row', 'col'), may hold values from 0 to 23, as said below
- block_counts: int32 [32, 16], P('row', 'col'), may hold values from 2 to 4, as said below
- cotangent: float32 [6144, 24576], P('row', 'col'), may hold values from -6 to 6
Outputs:
- hidden: bfloat16 [6144, 24576], P(('row', 'col'))
- input_grad: bfloat16 [6144, 8192], P('row', 'col')
- block_grads: bfloat16 [32, 16, 4, 128, 128], P('row', 'col')
The draws below stay inside these ranges and needn't reach their ends.
Inputs may be any that keep to these rules, and one draw needn't show every extreme that they name: `block_slots`: within one tile the 4 slot positions are distinct; slots from block_counts onward are unused and their blocks are arbitrary. `block_counts`: each tile uses at least half of its 4 slots (rounded down); some tile uses all 4.
All inputs are finite; a program needn't handle non-finite values.
Results may differ from the reference program's by a relative error of at most 0.022.
Values may be sent and summed in bfloat16 or wider, within the bound.
A program may use at most 64 MiB of HBM per device.

```python
import math
import jax
import jax.numpy as jnp
from jax import lax

D = 8192
FF = 24576
BLK = 128
TOK_ROW = 192
TOKENS = 6144
ROW_BLOCKS = 2
COL_BLOCKS = 12
HID_TILE = 1536
CAP = 4
N_ROW = 32
N_COL = 16


def draw_block_slots(key, part):
    key = jax.random.fold_in(key, 11)
    slot_total = ROW_BLOCKS * COL_BLOCKS
    scores = jax.random.randint(key, (N_ROW, N_COL, slot_total), 0, 1 << 20)
    scores = scores * slot_total + jnp.arange(slot_total, dtype=jnp.int32)
    top_scores, chosen = lax.top_k(scores, CAP)
    return chosen.astype(jnp.int32)


def draw_block_counts(key, part):
    key = jax.random.fold_in(key, 23)
    first_key, second_key = jax.random.split(key)
    counts = jax.random.randint(first_key, (N_ROW, N_COL), CAP // 2, CAP + 1)
    chosen = jax.random.randint(second_key, (), 0, N_ROW * N_COL)
    places = jnp.arange(N_ROW * N_COL, dtype=jnp.int32).reshape(N_ROW, N_COL)
    return jnp.where(places == chosen, CAP, counts).astype(jnp.int32)


def level_of(stream_key, extent, shards, least, largest):
    def one(position, shards_of):
        draws = jax.random.uniform(jax.random.fold_in(jax.random.fold_in(stream_key, 6), position), (shards_of,), jnp.float32, least / len(shards), largest / len(shards))
        return jnp.repeat(jnp.exp(draws), extent[position] // shards_of).reshape((-1,) + (1,) * (len(extent) - position - 1))

    level = one(*shards[0])
    for cut in shards[1:]:
        level = level * one(*cut)
    return level


def gaussian(rng, shape, deviation, reach, cuts=(), kind=jnp.bfloat16):
    entries = deviation * jax.random.normal(rng, shape, jnp.float32)
    if cuts:
        entries = entries * level_of(rng, shape, cuts, -0.22, 0.18)
    return jnp.clip(entries, -reach, reach).astype(kind)


def setup_inputs(seed: int = 0) -> dict:
    key_list = jax.random.split(jax.random.key(seed), 6)
    tokens = gaussian(key_list[0], (TOKENS, D), 1.0, 6.0, ((0, 32), (1, 16)))
    weight_blocks = gaussian(key_list[1], (N_ROW, N_COL, CAP, BLK, BLK), (D // 8) ** -0.5, 0.1875, ((0, 32), (1, 16)))
    block_slots = draw_block_slots(jax.random.fold_in(key_list[5], 71), 0)
    block_counts = draw_block_counts(jax.random.fold_in(key_list[5], 71), 0)
    cotangent = gaussian(key_list[4], (TOKENS, FF), 1.0, 6.0, ((0, 32), (1, 16)), jnp.float32)
    return {"tokens": tokens, "weight_blocks": weight_blocks, "block_slots": block_slots, "block_counts": block_counts, "cotangent": cotangent}


gelu_scale = 0.7978845608028654
cubic_term = 0.044715

def gelu_pair(pre_act):
    inner = gelu_scale * (pre_act + cubic_term * pre_act * pre_act * pre_act)
    tanh_value = jnp.tanh(inner)
    activated = 0.5 * pre_act * (1.0 + tanh_value)
    derivative = 0.5 * (1.0 + tanh_value) + 0.5 * pre_act * (1.0 - tanh_value * tanh_value) * gelu_scale * (1.0 + 3.0 * cubic_term * pre_act * pre_act)
    return (activated, derivative)

def block_tables(slot_table, count_table, first_row, row_blocks, col_blocks):
    grid_row = first_row + jnp.arange(slot_table.shape[0], dtype=jnp.int32)
    block_rows = grid_row[:, None] * row_blocks + slot_table // col_blocks
    block_cols = slot_table % col_blocks
    usable = jnp.arange(slot_table.shape[1], dtype=jnp.int32)[None, :] < count_table[:, None]
    return (block_rows.reshape(-1), block_cols.reshape(-1), usable.reshape(-1))

def reference(tokens, weight_blocks, block_slots, block_counts, cotangent):
    block_depth = D // BLK
    token_blocks = tokens.reshape(TOKENS, block_depth, BLK)
    grad_scale = 1.0 / math.sqrt(TOKENS)
    columns = (jnp.transpose(weight_blocks, (1, 0, 2, 3, 4)), jnp.transpose(block_slots, (1, 0, 2)), jnp.transpose(block_counts, (1, 0)), jnp.transpose(cotangent.reshape(TOKENS, N_COL, HID_TILE), (1, 0, 2)))

    def column_group(running, member):
        stored, slot_table, count_table, grad_out = member
        block_rows, block_cols, usable = block_tables(slot_table, count_table, 0, ROW_BLOCKS, COL_BLOCKS)
        flattened = stored.reshape(-1, BLK, BLK)
        weights = (flattened * usable[:, None, None].astype(flattened.dtype)).astype(jnp.float32)
        picked = token_blocks[:, block_rows, :].astype(jnp.float32)
        product = jnp.einsum('tnk,nkm->tnm', picked, weights)
        pre_act = jnp.zeros((TOKENS, COL_BLOCKS, BLK), jnp.float32).at[:, block_cols, :].add(product)
        activated, derivative = gelu_pair(pre_act.reshape(TOKENS, HID_TILE))
        hidden_part = activated.astype(jnp.bfloat16)
        grad_pre = (grad_out * derivative).astype(jnp.bfloat16)
        grad_picked = grad_pre.reshape(TOKENS, COL_BLOCKS, BLK)[:, block_cols, :].astype(jnp.float32)
        back_sum = jnp.einsum('tnm,nkm->tnk', grad_picked, weights)
        partial_value = jnp.zeros((TOKENS, block_depth, BLK), jnp.float32).at[:, block_rows, :].add(back_sum)
        rounded = lax.optimization_barrier(partial_value.reshape(TOKENS, D).astype(jnp.bfloat16))
        running = running + rounded.astype(jnp.float32)

        def token_group(summed, operands):
            partial_term = jnp.einsum('tnk,tnm->nkm', operands[0], operands[1])
            rounded_term = lax.optimization_barrier(partial_term.astype(jnp.bfloat16))
            return (summed + rounded_term.astype(jnp.float32), None)
        block_total = block_rows.shape[0]
        grouped_tokens = picked.reshape(N_ROW, TOK_ROW, block_total, BLK)
        grouped_grads = grad_picked.reshape(N_ROW, TOK_ROW, block_total, BLK)
        summed, unused = lax.scan(token_group, jnp.zeros((block_total, BLK, BLK), jnp.float32), (grouped_tokens, grouped_grads))
        gradients = (summed * grad_scale * usable[:, None, None].astype(jnp.float32)).astype(jnp.bfloat16)
        return (running, (hidden_part, gradients.reshape(N_ROW, CAP, BLK, BLK)))
    final_sum, outputs = lax.scan(column_group, jnp.zeros((TOKENS, D), jnp.float32), columns)
    hidden = jnp.transpose(outputs[0], (1, 0, 2)).reshape(TOKENS, FF)
    input_grad = final_sum.astype(jnp.bfloat16)
    block_grads = jnp.transpose(outputs[1], (1, 0, 2, 3, 4))
    return (hidden, input_grad, block_grads)
```

```python
import math

import jax
import jax.numpy as jnp
from jax import lax
from jax.experimental import pallas as pl
from jax.experimental.pallas import tpu as pltpu
from jax.sharding import PartitionSpec as P

MESH = pl.DeviceIdType.MESH
ny, nx, nz, nk = 8, 4, 8, 2


def wrap(v, n):
    return lax.rem(v + n, n)


def position():
    r = lax.axis_index("row")
    c = lax.axis_index("col")
    return r // nx, lax.rem(r, nx), c // nk, lax.rem(c, nk)


def device(y, x, z, k):
    return (y * nx + x, z * nk + k)


class Mail:
    def __init__(self, send_sem, recv_sem):
        self.send_sem, self.recv_sem = send_sem, recv_sem
        self.ids = {}
        self.sent = []

    def slot(self, name):
        return self.ids.setdefault(name, len(self.ids))

    def copy(self, name, src, dst, to):
        i = self.slot(name)
        return pltpu.make_async_remote_copy(
            src_ref=src, dst_ref=dst, send_sem=self.send_sem.at[i], recv_sem=self.recv_sem.at[i],
            device_id=to, device_id_type=MESH,
        )

    def send(self, name, src, dst, to):
        c = self.copy(name, src, dst, to)
        c.start()
        self.sent.append(c)

    def recv(self, name, dst, to):
        self.copy(name, dst, dst, to).wait_recv()

    def drain(self):
        for c in self.sent:
            c.wait_send()
        self.sent = []


def enter(y, x, z, k, col_all=False):
    bar = pltpu.get_barrier_semaphore()
    peers = [
        device(wrap(y + 1, ny), x, z, k), device(wrap(y - 1, ny), x, z, k),
        device(y, wrap(x + 1, nx), z, k), device(y, wrap(x - 1, nx), z, k),
    ]
    if col_all:
        peers += [device(y, x, wrap(z + i, nz), lax.rem(k + j, nk)) for i in range(nz) for j in range(nk) if i or j]
    else:
        peers += [device(y, x, wrap(z + 1, nz), k), device(y, x, wrap(z - 1, nz), k), device(y, x, z, 1 - k)]
    for p in peers:
        pl.semaphore_signal(bar, inc=1, device_id=p, device_id_type=MESH)
    pl.semaphore_wait(bar, len(peers))


wrows = 528
cut = 208


def gather_weights_tokens(mail, y, x, z, k, w_ref, tok_ref, W, T):
    A = pl.ds(0, cut)
    B = pl.ds(cut, wrows - cut)
    ha = {1: pl.ds(0, 112), -1: pl.ds(112, 96)}
    hb = {1: pl.ds(cut, 160), -1: pl.ds(cut + 160, 160)}
    ht = {1: pl.ds(0, 96), -1: pl.ds(96, 96)}
    both = (1, -1)
    ydev = {s: device(wrap(y + s, ny), x, z, k) for s in both}
    xdev = {s: device(y, wrap(x + s, nx), z, k) for s in both}
    zdev = {s: device(y, x, wrap(z + s, nz), k) for s in both}
    kdev = device(y, x, z, 1 - k)
    yy = lambda d: wrap(y + d, ny)
    xx = lambda d: wrap(x + d, nx)
    zz = lambda d: wrap(z + d, nz)

    for s in both:
        mail.send(f"by1{s}", w_ref.at[B], W.at[y, x, B], ydev[s])
        mail.send(f"ax1{s}", w_ref.at[A], W.at[y, x, A], xdev[s])
        mail.send(f"tz1{s}", tok_ref, T.at[z, k], zdev[s])
    for s in both:
        mail.send(f"ay1{s}x0", w_ref.at[A], W.at[y, x, A], ydev[s])
        mail.send(f"bx1{s}y0", w_ref.at[B], W.at[y, x, B], xdev[s])
    mail.send("tk0", tok_ref, T.at[z, k], kdev)

    def tz(hop):
        for s in both:
            piece = T.at[zz(-s * hop), k]
            mail.recv(f"tz{hop}{s}", piece, zdev[s])
            if hop < 3:
                mail.send(f"tz{hop + 1}{s}", piece, piece, zdev[s])
            else:
                half = T.at[zz(-s * hop), k, ht[s]]
                mail.send(f"tz4{s}", half, half, zdev[s])
            mail.send(f"tk{-s * hop}", piece, piece, kdev)

    def tz4():
        for s in both:
            half = T.at[zz(4), k, ht[s]]
            mail.recv(f"tz4{s}", half, zdev[s])
        piece = T.at[zz(4), k]
        mail.send("tk4", piece, piece, kdev)

    def by(hop):
        for s in both:
            piece = W.at[yy(-s * hop), x, B]
            mail.recv(f"by{hop}{s}", piece, ydev[s])
            if hop < 3:
                mail.send(f"by{hop + 1}{s}", piece, piece, ydev[s])
            else:
                half = W.at[yy(-s * hop), x, hb[s]]
                mail.send(f"by4{s}", half, half, ydev[s])
        for s in both:
            piece = W.at[yy(-s * hop), x, B]
            for t in both:
                mail.send(f"bx1{t}y{-s * hop}", piece, piece, xdev[t])

    def by4():
        for s in both:
            mail.recv(f"by4{s}", W.at[yy(4), x, hb[s]], ydev[s])
        piece = W.at[yy(4), x, B]
        for t in both:
            mail.send(f"bx1{t}y4", piece, piece, xdev[t])

    def bx1(d):
        for t in both:
            mail.recv(f"bx1{t}y{d}", W.at[yy(d), xx(-t), B], xdev[t])
            half = W.at[yy(d), xx(-t), hb[t]]
            mail.send(f"bx2{t}y{d}", half, half, xdev[t])

    def bx2(d):
        for t in both:
            mail.recv(f"bx2{t}y{d}", W.at[yy(d), xx(2), hb[t]], xdev[t])

    def ax1():
        for t in both:
            mail.recv(f"ax1{t}", W.at[y, xx(-t), A], xdev[t])
            half = W.at[y, xx(-t), ha[t]]
            mail.send(f"ax2{t}", half, half, xdev[t])
        for t in both:
            piece = W.at[y, xx(-t), A]
            for s in both:
                mail.send(f"ay1{s}x{-t}", piece, piece, ydev[s])

    def ax2():
        for t in both:
            mail.recv(f"ax2{t}", W.at[y, xx(2), ha[t]], xdev[t])
        piece = W.at[y, xx(2), A]
        for s in both:
            mail.send(f"ay1{s}x2", piece, piece, ydev[s])

    def ay1():
        for s in both:
            for e in (0, 1, -1, 2):
                mail.recv(f"ay1{s}x{e}", W.at[yy(-s), xx(e), A], ydev[s])
            piece = W.at[yy(-s), :, A]
            mail.send(f"ay2{s}", piece, piece, ydev[s])

    def ay(hop):
        for s in both:
            piece = W.at[yy(-s * hop), :, A]
            mail.recv(f"ay{hop}{s}", piece, ydev[s])
            if hop < 3:
                mail.send(f"ay{hop + 1}{s}", piece, piece, ydev[s])
            else:
                half = W.at[yy(-s * hop), :, ha[s]]
                mail.send(f"ay4{s}", half, half, ydev[s])

    def ay4():
        for s in both:
            mail.recv(f"ay4{s}", W.at[yy(4), :, ha[s]], ydev[s])

    ax1(); by(1); tz(1); ax2(); bx1(0); by(2); tz(2); ay1()
    bx1(1); bx1(-1); by(3); tz(3); ay(2); bx1(2); bx1(-2); by4(); tz4()
    bx1(3); bx1(-3); ay(3); bx1(4)
    for d in (0, 1, -1, 2, -2, 3, -3, 4):
        bx2(d)
    ay4()
    for d in (0, 1, -1, 2, -2, 3, -3, 4):
        mail.recv(f"tk{d}", T.at[zz(d), 1 - k], kdev)


def k1_body(w_ref, tok_ref, W, T, send_sem, recv_sem, own_sem):
    y, x, z, k = position()
    own = [pltpu.make_async_copy(w_ref, W.at[y, x], own_sem.at[0]), pltpu.make_async_copy(tok_ref, T.at[z, k], own_sem.at[1])]
    for c in own:
        c.start()
    enter(y, x, z, k)
    mail = Mail(send_sem, recv_sem)
    gather_weights_tokens(mail, y, x, z, k, w_ref, tok_ref, W, T)
    for c in own:
        c.wait()
    mail.drain()


def k1(w, tok, cid=0, name="gather"):
    n = 96
    vm = pl.BlockSpec(memory_space=pltpu.VMEM)
    return pl.pallas_call(
        k1_body, name=name,
        out_shape=(jax.ShapeDtypeStruct((ny, nx, wrows, 128), jnp.bfloat16), jax.ShapeDtypeStruct((nz, nk, 192, 512), jnp.bfloat16)),
        in_specs=[vm, vm], out_specs=(vm, vm),
        scratch_shapes=[pltpu.SemaphoreType.DMA((n,)), pltpu.SemaphoreType.DMA((n,)), pltpu.SemaphoreType.DMA((2,))],
        compiler_params=pltpu.CompilerParams(collective_id=cid, has_side_effects=True, vmem_limit_bytes=48 * 2**20),
    )(w, tok)

gelu_scale = 0.7978845608028654
cubic_term = 0.044715
far = (4, 3, -3, 2, -2, 1, -1, 0)


def gelu_pair(v):
    inner = gelu_scale * (v + cubic_term * v * v * v)
    th = jnp.tanh(inner)
    act = 0.5 * v * (1.0 + th)
    der = 0.5 * (1.0 + th) + 0.5 * v * (1.0 - th * th) * gelu_scale * (1.0 + 3.0 * cubic_term * v * v)
    return act, der


def wide_tile(W, slots, y, x, a):
    top, bottom = [], []
    for s in range(4):
        w = W[y, x, s * 128:(s + 1) * 128, :]
        upper = slots[a * 4 + s] < 12
        zero = jnp.zeros_like(w)
        top.append(jnp.where(upper, w, zero))
        bottom.append(jnp.where(upper, zero, w))
    return jnp.concatenate([jnp.concatenate(top, 1), jnp.concatenate(bottom, 1)], 0)


def k2_body(slots, W, T, cot, H, gp, pre, S, Hs):
    pre[...] = jnp.zeros_like(pre)

    def tile(a, _):
        wide = wide_tile(W, slots, a // 4, lax.rem(a, 4), a)
        tok = T[a // 4, lax.rem(a // 2, 2), :, pl.ds(pl.multiple_of(lax.rem(a, 2) * 256, 256), 256)]
        P = jnp.dot(tok, wide, preferred_element_type=jnp.float32)
        for s in range(4):
            j = lax.rem(slots[a * 4 + s], 12)
            pre[j] += P[:, s * 128:(s + 1) * 128]
        return 0

    lax.fori_loop(0, 32, tile, 0)
    for j in range(12):
        act, der = gelu_pair(pre[j])
        gp[j] = (cot[:, j * 128:(j + 1) * 128] * der).astype(jnp.bfloat16)
        S[...] = act
        for c in range(16):
            Hs[c, (j // 6) * 8:(j // 6) * 8 + 8, (j % 6) * 128:(j % 6 + 1) * 128] = S[12 * c:12 * c + 8]
            Hs[c, (j // 3) * 4:(j // 3) * 4 + 4, 768 + (j % 3) * 128:768 + (j % 3 + 1) * 128] = S[12 * c + 8:12 * c + 12]
    for c in range(16):
        H[c] = Hs[c].astype(jnp.bfloat16)


def k2(slots, W, T, cot):
    vm = pl.BlockSpec(memory_space=pltpu.VMEM)
    return pl.pallas_call(
        k2_body, name="forward",
        out_shape=(jax.ShapeDtypeStruct((16, 16, 1152), jnp.bfloat16), jax.ShapeDtypeStruct((12, 192, 128), jnp.bfloat16)),
        in_specs=[pl.BlockSpec(memory_space=pltpu.SMEM), vm, vm, vm], out_specs=(vm, vm),
        scratch_shapes=[pltpu.VMEM((12, 192, 128), jnp.float32), pltpu.VMEM((192, 128), jnp.float32), pltpu.VMEM((16, 16, 1152), jnp.float32)],
        compiler_params=pltpu.CompilerParams(vmem_limit_bytes=48 * 2**20),
    )(slots, W, T, cot)


acut = 208


def k3_body(slots, count, W, T, gp, H, HR, dx_out, dw_out, G, D, Ray, Rax, Rbx, Rby, Rk, Rz, send_sem, recv_sem, own_sem):
    y, x, z, k = position()
    c_me = z * 2 + k
    keep = pltpu.make_async_copy(H.at[c_me], HR.at[c_me], own_sem.at[0])
    keep.start()
    enter(y, x, z, k, col_all=True)
    mail = Mail(send_sem, recv_sem)
    both = (1, -1)
    brows = 512 - acut
    A = pl.ds(0, acut)
    B = pl.ds(acut, brows)
    ha = {1: pl.ds(0, 112), -1: pl.ds(112, 96)}
    hb = {1: pl.ds(acut, 160), -1: pl.ds(acut + 160, brows - 160)}
    hr = {1: pl.ds(0, 160), -1: pl.ds(160, brows - 160)}
    ht = {1: pl.ds(0, 96), -1: pl.ds(96, 96)}
    ydev = {s: device(wrap(y + s, ny), x, z, k) for s in both}
    xdev = {s: device(y, wrap(x + s, nx), z, k) for s in both}
    zdev = {s: device(y, x, wrap(z + s, nz), k) for s in both}
    kdev = device(y, x, z, 1 - k)
    yy = lambda d: wrap(y + d, ny)
    xx = lambda d: wrap(x + d, nx)
    zz = lambda d: wrap(z + d, nz)

    def grad_cat(a):
        return jnp.concatenate([gp[lax.rem(slots[a * 4 + s], 12)] for s in range(4)], 1)

    def terms(d):
        def tile(xi, _):
            yi = yy(d)
            a = yi * 4 + xi
            tok = T[a // 4, lax.rem(a // 2, 2), :, pl.ds(pl.multiple_of(lax.rem(a, 2) * 256, 256), 256)]
            full = lax.dot_general(tok, grad_cat(a), (((0,), (0,)), ((), ())), preferred_element_type=jnp.float32)
            for s in range(4):
                upper = slots[a * 4 + s] < 12
                part = full[:, s * 128:(s + 1) * 128]
                G[yi, xi, s * 128:(s + 1) * 128, :] = jnp.where(upper, part[:128], part[128:]).astype(jnp.bfloat16)
            return 0
        lax.fori_loop(0, 4, tile, 0)

    def partial(d):
        def tile(i, _):
            zi = zz(d)
            a = zi * 4 + i
            wide = wide_tile(W, slots, a // 4, lax.rem(a, 4), a)
            out = lax.dot_general(grad_cat(a), wide, (((1,), (1,)), ((), ())), preferred_element_type=jnp.float32)
            D[zi, i // 2, :, pl.ds(pl.multiple_of(lax.rem(i, 2) * 256, 256), 256)] = out.astype(jnp.bfloat16)
            return 0
        lax.fori_loop(0, 4, tile, 0)

    def send_hidden(dz):
        for dk in range(2):
            if dz == 0 and dk == 0:
                continue
            to = (zz(dz), lax.rem(k + dk, 2))
            mail.send(f"h{dz % 8}{dk}", H.at[to[0] * 2 + to[1]], HR.at[c_me], device(y, x, to[0], to[1]))

    def recv_hidden(dz):
        for dk in range(2):
            if dz == 0 and dk == 0:
                continue
            src = zz(-dz) * 2 + lax.rem(k + dk, 2)
            mail.recv(f"h{dz % 8}{dk}", HR.at[src], kdev)

    def ay1():
        for s in both:
            mail.send(f"ay1{s}", G.at[yy(4), :, ha[s]], Ray.at[(1 - s) // 2, 0, :, ha[s]], ydev[s])

    def ay(hop):
        for s in both:
            i = (1 - s) // 2
            yi = yy(s * (5 - hop))
            rows = ha[s] if hop == 2 else A
            mail.recv(f"ay{hop - 1}{s}", Ray.at[i, hop - 2, :, rows], ydev[s])
            G[yi, :, rows, :] = G[yi, :, rows, :] + Ray[i, hop - 2, :, rows, :]
            mail.send(f"ay{hop}{s}", G.at[yi, :, A], Ray.at[i, hop - 1, :, A], ydev[s])

    def ay_end():
        for s in both:
            mail.recv(f"ay4{s}", Ray.at[(1 - s) // 2, 3, :, A], ydev[s])
        f = jnp.float32
        G[y, :, A, :] = (G[y, :, A, :].astype(f) + Ray[0, 3, :, A, :].astype(f) + Ray[1, 3, :, A, :].astype(f)).astype(jnp.bfloat16)

    def ax1():
        for t in both:
            mail.send(f"ax1{t}", G.at[y, xx(2), ha[t]], Rax.at[(1 - t) // 2, 0, ha[t]], xdev[t])

    def ax2():
        for t in both:
            i = (1 - t) // 2
            mail.recv(f"ax1{t}", Rax.at[i, 0, ha[t]], xdev[t])
            G[y, xx(t), ha[t], :] = G[y, xx(t), ha[t], :] + Rax[i, 0, ha[t], :]
            mail.send(f"ax2{t}", G.at[y, xx(t), A], Rax.at[i, 1], xdev[t])

    def finish(rows, r0, r1):
        f = jnp.float32
        total = G[y, x, rows, :].astype(f) + r0.astype(f) + r1.astype(f)
        block = lax.broadcasted_iota(jnp.int32, total.shape, 0) + rows.start
        usable = block < count[0] * 128
        dw_out[rows, :] = jnp.where(usable, total * (1.0 / math.sqrt(6144)), 0.0).astype(jnp.bfloat16)

    def ax_end():
        for t in both:
            mail.recv(f"ax2{t}", Rax.at[(1 - t) // 2, 1], xdev[t])
        finish(A, Rax[0, 1], Rax[1, 1])

    def bx1(d):
        for t in both:
            mail.send(f"bx1{t}y{d}", G.at[yy(d), xx(2), hb[t]], Rbx.at[(1 - t) // 2, 0, yy(d), hr[t]], xdev[t])

    def bx2(d):
        for t in both:
            i = (1 - t) // 2
            mail.recv(f"bx1{t}y{d}", Rbx.at[i, 0, yy(d), hr[t]], xdev[t])
            G[yy(d), xx(t), hb[t], :] = G[yy(d), xx(t), hb[t], :] + Rbx[i, 0, yy(d), hr[t], :]
            mail.send(f"bx2{t}y{d}", G.at[yy(d), xx(t), B], Rbx.at[i, 1, yy(d)], xdev[t])

    def bx_end(d):
        for t in both:
            mail.recv(f"bx2{t}y{d}", Rbx.at[(1 - t) // 2, 1, yy(d)], xdev[t])
        f = jnp.float32
        G[yy(d), x, B, :] = (G[yy(d), x, B, :].astype(f) + Rbx[0, 1, yy(d)].astype(f) + Rbx[1, 1, yy(d)].astype(f)).astype(jnp.bfloat16)

    def by1():
        for s in both:
            mail.send(f"by1{s}", G.at[yy(4), x, hb[s]], Rby.at[(1 - s) // 2, 0, hr[s]], ydev[s])

    def by(hop):
        for s in both:
            i = (1 - s) // 2
            yi = yy(s * (5 - hop))
            rows, inner = (hb[s], hr[s]) if hop == 2 else (B, pl.ds(0, brows))
            mail.recv(f"by{hop - 1}{s}", Rby.at[i, hop - 2, inner], ydev[s])
            G[yi, x, rows, :] = G[yi, x, rows, :] + Rby[i, hop - 2, inner, :]
            mail.send(f"by{hop}{s}", G.at[yi, x, B], Rby.at[i, hop - 1], ydev[s])

    def by_end():
        for s in both:
            mail.recv(f"by4{s}", Rby.at[(1 - s) // 2, 3], ydev[s])
        finish(B, Rby[0, 3], Rby[1, 3])

    def dk_send(d):
        mail.send(f"dk{d}", D.at[zz(d), 1 - k], Rk.at[zz(d)], kdev)

    def dk_add(d):
        mail.recv(f"dk{d}", Rk.at[zz(d)], kdev)
        D[zz(d), k] = D[zz(d), k] + Rk[zz(d)]

    def dz1():
        dk_add(4)
        for s in both:
            mail.send(f"dz1{s}", D.at[zz(4), k, ht[s]], Rz.at[(1 - s) // 2, 0, ht[s]], zdev[s])

    def dz(hop):
        for s in both:
            i = (1 - s) // 2
            zi = zz(s * (5 - hop))
            dk_add(s * (5 - hop))
            rows = ht[s] if hop == 2 else pl.ds(0, 192)
            mail.recv(f"dz{hop - 1}{s}", Rz.at[i, hop - 2, rows], zdev[s])
            D[zi, k, rows, :] = D[zi, k, rows, :] + Rz[i, hop - 2, rows, :]
            mail.send(f"dz{hop}{s}", D.at[zi, k], Rz.at[i, hop - 1], zdev[s])

    def dz_end():
        dk_add(0)
        for s in both:
            mail.recv(f"dz4{s}", Rz.at[(1 - s) // 2, 3], zdev[s])
        f = jnp.float32
        dx_out[...] = (D[z, k].astype(f) + Rz[0, 3].astype(f) + Rz[1, 3].astype(f)).astype(jnp.bfloat16)

    terms(4); bx1(4); ay1()
    partial(4); dk_send(4)
    send_hidden(4); send_hidden(3); send_hidden(-3)
    terms(3); bx1(3); terms(-3); bx1(-3)
    partial(3); dk_send(3); partial(-3); dk_send(-3)
    bx2(4); dz1(); ay(2)
    terms(2); bx1(2); terms(-2); bx1(-2)
    bx2(3); bx2(-3)
    partial(2); dk_send(2); partial(-2); dk_send(-2)
    dz(2)
    bx_end(4); by1()
    send_hidden(2); send_hidden(-2)
    terms(1); bx1(1); terms(-1); bx1(-1)
    ay(3)
    bx2(2); bx2(-2); bx_end(3); bx_end(-3); by(2)
    partial(1); dk_send(1); partial(-1); dk_send(-1)
    dz(3)
    send_hidden(1); send_hidden(-1); send_hidden(0)
    terms(0); bx1(0); partial(0); dk_send(0)
    ay(4)
    bx2(1); bx2(-1); bx_end(2); bx_end(-2); by(3)
    dz(4)
    bx2(0); ay_end(); ax1(); bx_end(1); bx_end(-1); by(4)
    ax2()
    bx_end(0)
    dz_end()
    ax_end()
    by_end()
    for d in far:
        recv_hidden(d)
    keep.wait()
    mail.drain()


def k3(slots, count, W, T, gp, H, cid=1):
    vm = pl.BlockSpec(memory_space=pltpu.VMEM)
    sm = pl.BlockSpec(memory_space=pltpu.SMEM)
    n = 100
    bf = jnp.bfloat16
    return pl.pallas_call(
        k3_body, name="backward",
        out_shape=(jax.ShapeDtypeStruct((16, 16, 1152), bf), jax.ShapeDtypeStruct((192, 512), bf), jax.ShapeDtypeStruct((512, 128), bf)),
        in_specs=[sm, sm, vm, vm, vm, vm], out_specs=(vm, vm, vm),
        scratch_shapes=[
            pltpu.VMEM((8, 4, 512, 128), bf), pltpu.VMEM((8, 2, 192, 512), bf),
            pltpu.VMEM((2, 4, 4, acut, 128), bf), pltpu.VMEM((2, 2, acut, 128), bf),
            pltpu.VMEM((2, 2, 8, 512 - acut, 128), bf), pltpu.VMEM((2, 4, 512 - acut, 128), bf),
            pltpu.VMEM((8, 192, 512), bf), pltpu.VMEM((2, 4, 192, 512), bf),
            pltpu.SemaphoreType.DMA((n,)), pltpu.SemaphoreType.DMA((n,)), pltpu.SemaphoreType.DMA((1,)),
        ],
        compiler_params=pltpu.CompilerParams(collective_id=cid, has_side_effects=True, vmem_limit_bytes=56 * 2**20),
    )(slots, count, W, T, gp, H)


def body(tokens, weight_blocks, block_slots, block_counts, cotangent):
    count = block_counts[0]
    usable = jnp.arange(4, dtype=jnp.int32) < count[0]
    w = jnp.where(usable[:, None, None], weight_blocks[0, 0], jnp.zeros((), jnp.bfloat16)).reshape(512, 128)
    tail = jnp.broadcast_to(block_slots[0, 0].astype(jnp.bfloat16)[:, None], (4, 128))
    packed = jnp.concatenate([w, tail, jnp.zeros((12, 128), jnp.bfloat16)], 0)
    W, T = k1(packed, tokens, cid=0)
    slots = W[:, :, 512:516, 0].astype(jnp.int32).reshape(128)
    H, gp = k2(slots, W, T, cotangent)
    HR, dx, dw = k3(slots, count, W, T, gp, H)
    upper = HR[:, :, :768].reshape(16, 2, 8, 768).transpose(2, 0, 1, 3).reshape(8, 24576)
    lower = HR[:, :, 768:].reshape(16, 4, 4, 384).transpose(2, 0, 1, 3).reshape(4, 24576)
    hidden = jnp.concatenate([upper, lower], 0)
    return hidden, dx, dw.reshape(1, 1, 4, 128, 128)


def solution(mesh):
    in_specs = (
        P("row", "col"),
        P("row", "col", None, None, None),
        P("row", "col", None),
        P("row", "col"),
        P("row", "col"),
    )
    out_specs = (P(("row", "col"), None), P("row", "col"), P("row", "col", None, None, None))
    return jax.shard_map(body, mesh=mesh, in_specs=in_specs, out_specs=out_specs, check_vma=False)
```

```python
import functools
import math

import jax
import jax.numpy as jnp
from jax import lax
from jax.experimental import pallas as pl
from jax.experimental.pallas import tpu as pltpu
from jax.sharding import PartitionSpec as P

MESH = pl.DeviceIdType.MESH
ny, nx, nz, nk = 8, 4, 8, 2
both = (1, -1)
f32, bf16 = jnp.float32, jnp.bfloat16

gelu_scale = 0.7978845608028654
cubic_term = 0.044715

wrows = 528
wcut = 208
acut = 208


def gelu_pair(v):
    inner = gelu_scale * (v + cubic_term * v * v * v)
    th = jnp.tanh(inner)
    act = 0.5 * v * (1.0 + th)
    der = 0.5 * (1.0 + th) + 0.5 * v * (1.0 - th * th) * gelu_scale * (1.0 + 3.0 * cubic_term * v * v)
    return act, der


def wrap(v, n):
    return lax.rem(v + n, n)


class Mail:
    def __init__(self, send_sem, recv_sem):
        self.send_sem, self.recv_sem = send_sem, recv_sem
        self.ids = {}
        self.sent = []

    def copy(self, name, src, dst, to):
        i = self.ids.setdefault(name, len(self.ids))
        return pltpu.make_async_remote_copy(
            src_ref=src, dst_ref=dst, send_sem=self.send_sem.at[i], recv_sem=self.recv_sem.at[i],
            device_id=to, device_id_type=MESH,
        )

    def send(self, name, src, dst, to):
        self.copy(name, src, dst, to).start()
        self.sent.append((name, tuple(src.shape)))

    def recv(self, name, dst, to):
        self.copy(name, dst, dst, to).wait_recv()

    def drain(self, like, to):
        for name, shape in self.sent:
            self.copy(name, like(shape), like(shape), to).wait_send()
        self.sent = []


def kernel_body(
    slot_ref, count_ref, w_ref, tok_ref, cot_ref,
    hid_out, dx_out, dw_out,
    W, T, cot, code_v, code, dense, pre, gp, act_s, Hs, H, HR, G, D,
    Ray, Rax, Rbx, Rby, Rk, Rz,
    send_sem, recv_sem, own_sem, code_sem,
):
    r_me, c_me = lax.axis_index("row"), lax.axis_index("col")
    y, x, z, k = r_me // nx, lax.rem(r_me, nx), c_me // nk, lax.rem(c_me, nk)

    def device(yi, xi, zi, ki):
        return (yi * nx + xi, zi * nk + ki)

    own = [
        pltpu.make_async_copy(w_ref, W.at[y, x, pl.ds(0, 512)], own_sem.at[0]),
        pltpu.make_async_copy(tok_ref, T.at[z, k], own_sem.at[1]),
        pltpu.make_async_copy(cot_ref, cot, own_sem.at[2]),
    ]
    for c in own:
        c.start()

    yy = lambda d: wrap(y + d, ny)
    xx = lambda d: wrap(x + d, nx)
    zz = lambda d: wrap(z + d, nz)
    ydev = {s: device(yy(s), x, z, k) for s in both}
    xdev = {s: device(y, xx(s), z, k) for s in both}
    zdev = {s: device(y, x, zz(s), k) for s in both}
    kdev = device(y, x, z, 1 - k)

    bar = pltpu.get_barrier_semaphore()
    peers = [ydev[1], ydev[-1], xdev[1], xdev[-1]]
    peers += [device(y, x, zz(i), lax.rem(k + j, nk)) for i in range(nz) for j in range(nk) if i or j]
    for p in peers:
        pl.semaphore_signal(bar, inc=1, device_id=p, device_id_type=MESH)

    line = lax.broadcasted_iota(jnp.int32, (16, 128), 0)
    numbers = jnp.zeros((16, 128), f32)
    for s in range(4):
        number = jnp.where(s < count_ref[0], slot_ref[s], slot_ref[s] + 24)
        numbers = jnp.where(line == s, number.astype(f32), numbers)
    W[y, x, 512:528, :] = numbers.astype(bf16)
    pre[...] = jnp.zeros_like(pre)
    own[0].wait()
    own[1].wait()
    pl.semaphore_wait(bar, len(peers))

    mail = Mail(send_sem, recv_sem)

    def like(shape):
        if shape[-1] == 512:
            return T.at[0, 0, pl.ds(0, shape[0])]
        if shape[-1] == 1152:
            return H.at[0]
        if len(shape) == 3:
            return W.at[0, pl.ds(0, shape[0]), pl.ds(0, shape[1])]
        return W.at[0, 0, pl.ds(0, shape[0])]

    A = pl.ds(0, wcut)
    B = pl.ds(wcut, wrows - wcut)
    ha = {1: pl.ds(0, 112), -1: pl.ds(112, wcut - 112)}
    hb = {1: pl.ds(wcut, 160), -1: pl.ds(wcut + 160, wrows - wcut - 160)}
    side = 1 - 2 * lax.rem(x, 2)
    pair = {0: pl.ds(2 * (x // 2), 2), 1: pl.ds(2 * (1 - x // 2), 2)}
    role_x = {0: x, 1: xx(side), 2: xx(-side), 3: xx(2)}
    chunk = {s: [pl.ds(48 * i, 48) for i in ((0, 1, 2, 3) if s == 1 else (2, 3, 0, 1))] for s in both}

    def first_sends():
        for s in both:
            mail.send(f"by1{s}", W.at[y, x, B], W.at[y, x, B], ydev[s])
            mail.send(f"ax1{s}", W.at[y, x, A], W.at[y, x, A], xdev[s])
        for i in range(4):
            for s in both:
                mail.send(f"tz1{s}c{i}", T.at[z, k, chunk[s][i]], T.at[z, k, chunk[s][i]], zdev[s])
        for s in both:
            mail.send(f"ay1{s}r0", W.at[y, x, A], W.at[y, x, A], ydev[s])
            mail.send(f"bx1{s}y0", W.at[y, x, B], W.at[y, x, B], xdev[s])
        mail.send("tk0", T.at[z, k], T.at[z, k], kdev)

    def tz(hop, lo, hi):
        for i in range(lo, hi):
            for s in both:
                piece = T.at[zz(-s * hop), k, chunk[s][i]]
                if hop < 4 or i < 2:
                    mail.recv(f"tz{hop}{s}c{i}", piece, zdev[s])
                if hop < 3 or (hop == 3 and i < 2):
                    mail.send(f"tz{hop + 1}{s}c{i}", piece, piece, zdev[s])

    def tk(*ds):
        for d in ds:
            mail.send(f"tk{d}", T.at[zz(d), k], T.at[zz(d), k], kdev)

    def tk_end():
        for d in (0, 1, -1, 2, -2, 3, -3, 4):
            mail.recv(f"tk{d}", T.at[zz(d), 1 - k], kdev)

    def by(hop):
        for s in both:
            piece = W.at[yy(-s * hop), x, B]
            mail.recv(f"by{hop}{s}", piece, ydev[s])
            if hop < 3:
                mail.send(f"by{hop + 1}{s}", piece, piece, ydev[s])
            else:
                half = W.at[yy(-s * hop), x, hb[s]]
                mail.send(f"by4{s}", half, half, ydev[s])
        for s in both:
            piece = W.at[yy(-s * hop), x, B]
            for t in both:
                mail.send(f"bx1{t}y{-s * hop}", piece, piece, xdev[t])

    def by4():
        for s in both:
            mail.recv(f"by4{s}", W.at[yy(4), x, hb[s]], ydev[s])
        piece = W.at[yy(4), x, B]
        for t in both:
            mail.send(f"bx1{t}y4", piece, piece, xdev[t])

    def bx1(d):
        for t in both:
            mail.recv(f"bx1{t}y{d}", W.at[yy(d), xx(-t), B], xdev[t])
            half = W.at[yy(d), xx(-t), hb[t]]
            mail.send(f"bx2{t}y{d}", half, half, xdev[t])

    def bx2(d):
        for t in both:
            mail.recv(f"bx2{t}y{d}", W.at[yy(d), xx(2), hb[t]], xdev[t])

    def ax1():
        for t in both:
            mail.recv(f"ax1{t}", W.at[y, xx(-t), A], xdev[t])
            half = W.at[y, xx(-t), ha[t]]
            mail.send(f"ax2{t}", half, half, xdev[t])
        for role in (1, 2):
            piece = W.at[y, role_x[role], A]
            for s in both:
                mail.send(f"ay1{s}r{role}", piece, piece, ydev[s])

    def ax2():
        for t in both:
            mail.recv(f"ax2{t}", W.at[y, xx(2), ha[t]], xdev[t])
        piece = W.at[y, xx(2), A]
        for s in both:
            mail.send(f"ay1{s}r3", piece, piece, ydev[s])

    def ay1(p):
        for s in both:
            for role in (2 * p, 2 * p + 1):
                mail.recv(f"ay1{s}r{role}", W.at[yy(-s), role_x[role], A], ydev[s])
            piece = W.at[yy(-s), pair[p], A]
            mail.send(f"ay2{s}p{p}", piece, piece, ydev[s])

    def ay(hop, p):
        for s in both:
            piece = W.at[yy(-s * hop), pair[p], A]
            mail.recv(f"ay{hop}{s}p{p}", piece, ydev[s])
            if hop == 2:
                mail.send(f"ay3{s}p{p}", piece, piece, ydev[s])
            else:
                half = W.at[yy(-s * hop), pair[p], ha[s]]
                mail.send(f"ay4{s}p{p}", half, half, ydev[s])

    def ay4():
        for p in range(2):
            for s in both:
                mail.recv(f"ay4{s}p{p}", W.at[yy(4), pair[p], ha[s]], ydev[s])

    def near_first(r):
        m = (r + 1) // 2
        return m * (2 * lax.rem(r, 2) - 1)

    def build(r):
        yi = wrap(y + near_first(r), ny)

        def tile(xi, _):
            rows = W[yi, xi, 512:528, :]
            code_v[yi, xi] = rows[:8].astype(f32).astype(jnp.int32)
            numbers = [jnp.broadcast_to(rows[s:s + 1, :], (16, 128)) for s in range(4)]
            blocks = [W[yi, xi, s * 128:(s + 1) * 128, :].reshape(8, 16, 128) for s in range(4)]
            for p in range(24):
                total = jnp.zeros((8, 16, 128), bf16)
                for s in range(4):
                    total = jnp.where((numbers[s] == p)[None], blocks[s], total)
                dense[yi, pl.ds(pl.multiple_of(xi * 256 + (p // 12) * 128, 128), 128), (p % 12) * 128:(p % 12 + 1) * 128] = total.reshape(128, 128)
            return 0

        lax.fori_loop(0, 4, tile, 0)
        pltpu.make_async_copy(code_v.at[yi], code.at[yi], code_sem.at[yi]).start()

    def apply(r):
        yi = wrap(y + near_first(r), ny)

        def part(j, _):
            cols = pl.ds(pl.multiple_of(j * 256, 256), 256)
            pre[:, cols] += jnp.dot(T[yi, 0], dense[yi, 0:512, cols], preferred_element_type=f32) + jnp.dot(
                T[yi, 1], dense[yi, 512:1024, cols], preferred_element_type=f32)
            return 0

        lax.fori_loop(0, 6, part, 0)

    first_sends()
    by(1); ax1(); tz(1, 0, 4); tk(1, -1); bx1(0); by(2); ax2(); ay1(0)

    def gather_round(r, _):
        @pl.when(r == 0)
        def _():
            tz(2, 0, 4); tk(2, -2); bx1(1); bx1(-1); by(3); ay1(1); ay(2, 0); bx2(0)

        @pl.when(r == 1)
        def _():
            tz(3, 0, 4); tk(3, -3); bx1(2); bx1(-2); by4(); ay(2, 1); bx2(1); bx2(-1)

        @pl.when(r == 3)
        def _():
            tz(4, 0, 2); tk(4); bx1(3); bx1(-3); ay(3, 0); bx2(2); bx2(-2)

        @pl.when(r == 5)
        def _():
            bx1(4); ay(3, 1); tk_end(); bx2(3); bx2(-3)

        @pl.when(r == 7)
        def _():
            bx2(4); ay4()

        build(r)

        @pl.when(r >= 5)
        def _():
            def two(i, _):
                apply(i)
                return 0
            lax.fori_loop(3 * (r - 5), jnp.minimum(3 * (r - 5) + 3, 8), two, 0)
        return 0

    lax.fori_loop(0, 8, gather_round, 0)
    own[2].wait()

    def activation(i, _):
        for q in range(4):
            j = 3 * q + i
            cols = pl.ds(pl.multiple_of(j * 128, 128), 128)
            act, der = gelu_pair(pre[:, cols])
            gp[j] = (cot[:, cols] * der).astype(bf16)
            act_s[...] = act
            upper = pl.ds(pl.multiple_of((3 * (q % 2) + i) * 128, 128), 128)
            lower = pl.ds(pl.multiple_of(768 + i * 128, 128), 128)
            for c in range(16):
                Hs[c, 8 * (q // 2):8 * (q // 2) + 8, upper] = act_s[12 * c:12 * c + 8]
                Hs[c, 4 * q:4 * q + 4, lower] = act_s[12 * c + 8:12 * c + 12]
        return 0

    lax.fori_loop(0, 3, activation, 0)
    H[...] = Hs[...].astype(bf16)
    keep = pltpu.make_async_copy(H.at[c_me], HR.at[c_me], own_sem.at[3])
    keep.start()

    def code_wait(g, _):
        pltpu.make_async_copy(code_v.at[g], code.at[g], code_sem.at[g]).wait()
        return 0

    lax.fori_loop(0, 8, code_wait, 0)

    brows = 512 - acut
    A = pl.ds(0, acut)
    B = pl.ds(acut, brows)
    ha2 = {1: pl.ds(0, 112), -1: pl.ds(112, acut - 112)}
    hb2 = {1: pl.ds(acut, 160), -1: pl.ds(acut + 160, brows - 160)}
    hr = {1: pl.ds(0, 160), -1: pl.ds(160, brows - 160)}
    ht = {1: pl.ds(0, 96), -1: pl.ds(96, 96)}

    def far_first(r):
        m = (r + 1) // 2
        return (4 - m) * (2 * lax.rem(r, 2) - 1)

    def grad_cat(g, i):
        return jnp.concatenate([gp[jnp.clip(lax.rem(code[g, i, s, 0], 12), 0, 11)] for s in range(4)], 1)

    def terms(r):
        yi = wrap(y + far_first(r), ny)
        for i in range(4):
            tok = T[yi, i // 2, :, (i % 2) * 256:(i % 2 + 1) * 256]
            full = lax.dot_general(tok, grad_cat(yi, i), (((0,), (0,)), ((), ())), preferred_element_type=f32)
            for s in range(4):
                part = full[:, s * 128:(s + 1) * 128]
                G[yi, i, s * 128:(s + 1) * 128, :] = jnp.where(code[yi, i, s, 0] < 12, part[:128], part[128:]).astype(bf16)

    def partial(r):
        zi = wrap(z + far_first(r), nz)
        for i in range(4):
            top, bottom = [], []
            for s in range(4):
                w = W[zi, i, s * 128:(s + 1) * 128, :]
                n = code[zi, i, s, 0]
                top.append(jnp.where(n < 12, w, jnp.zeros_like(w)))
                bottom.append(jnp.where((n >= 12) & (n < 24), w, jnp.zeros_like(w)))
            wide = jnp.concatenate([jnp.concatenate(top, 1), jnp.concatenate(bottom, 1)], 0)
            out = lax.dot_general(grad_cat(zi, i), wide, (((1,), (1,)), ((), ())), preferred_element_type=f32)
            D[zi, i // 2, :, (i % 2) * 256:(i % 2 + 1) * 256] = out.astype(bf16)

    def send_hidden(*ds):
        for dz in ds:
            for dk in range(2):
                if dz or dk:
                    zi, ki = zz(dz), lax.rem(k + dk, 2)
                    mail.send(f"h{dz % 8}{dk}", H.at[zi * 2 + ki], HR.at[c_me], device(y, x, zi, ki))

    def recv_hidden(*ds):
        for dz in ds:
            for dk in range(2):
                if dz or dk:
                    mail.recv(f"h{dz % 8}{dk}", HR.at[zz(-dz) * 2 + lax.rem(k + dk, 2)], kdev)

    xpair = [pl.ds(0, 2), pl.ds(2, 2)]

    def gy1(p):
        for s in both:
            mail.send(f"gy1{s}p{p}", G.at[yy(4), xpair[p], ha2[s]], Ray.at[(1 - s) // 2, 0, xpair[p], ha2[s]], ydev[s])

    def gy(hop, p):
        for s in both:
            i, yi, xp = (1 - s) // 2, yy(s * (5 - hop)), xpair[p]
            rows = ha2[s] if hop == 2 else A
            mail.recv(f"gy{hop - 1}{s}p{p}", Ray.at[i, hop - 2, xp, rows], ydev[s])
            G[yi, xp, rows, :] = G[yi, xp, rows, :] + Ray[i, hop - 2, xp, rows, :]
            mail.send(f"gy{hop}{s}p{p}", G.at[yi, xp, A], Ray.at[i, hop - 1, xp, A], ydev[s])

    def gy_end(p):
        for s in both:
            mail.recv(f"gy4{s}p{p}", Ray.at[(1 - s) // 2, 3, xpair[p], A], ydev[s])
        xp = xpair[p]
        G[y, xp, A, :] = (G[y, xp, A, :].astype(f32) + Ray[0, 3, xp, A, :].astype(f32) + Ray[1, 3, xp, A, :].astype(f32)).astype(bf16)

    def gx1():
        for t in both:
            mail.send(f"gx1{t}", G.at[y, xx(2), ha2[t]], Rax.at[(1 - t) // 2, 0, ha2[t]], xdev[t])

    def gx2():
        for t in both:
            i = (1 - t) // 2
            mail.recv(f"gx1{t}", Rax.at[i, 0, ha2[t]], xdev[t])
            G[y, xx(t), ha2[t], :] = G[y, xx(t), ha2[t], :] + Rax[i, 0, ha2[t], :]
            mail.send(f"gx2{t}", G.at[y, xx(t), A], Rax.at[i, 1], xdev[t])

    def finish(rows, r0, r1):
        total = G[y, x, rows, :].astype(f32) + r0.astype(f32) + r1.astype(f32)
        row = lax.broadcasted_iota(jnp.int32, total.shape, 0) + rows.start
        usable = row < count_ref[0] * 128
        dw_out[rows, :] = jnp.where(usable, total * (1.0 / math.sqrt(6144)), 0.0).astype(bf16)

    def gx_end():
        for t in both:
            mail.recv(f"gx2{t}", Rax.at[(1 - t) // 2, 1], xdev[t])
        finish(A, Rax[0, 1], Rax[1, 1])

    def qx1(d):
        for t in both:
            mail.send(f"qx1{t}y{d}", G.at[yy(d), xx(2), hb2[t]], Rbx.at[(1 - t) // 2, 0, yy(d), hr[t]], xdev[t])

    def qx2(d):
        for t in both:
            i = (1 - t) // 2
            mail.recv(f"qx1{t}y{d}", Rbx.at[i, 0, yy(d), hr[t]], xdev[t])
            G[yy(d), xx(t), hb2[t], :] = G[yy(d), xx(t), hb2[t], :] + Rbx[i, 0, yy(d), hr[t], :]
            mail.send(f"qx2{t}y{d}", G.at[yy(d), xx(t), B], Rbx.at[i, 1, yy(d)], xdev[t])

    def qx_end(d):
        for t in both:
            mail.recv(f"qx2{t}y{d}", Rbx.at[(1 - t) // 2, 1, yy(d)], xdev[t])
        G[yy(d), x, B, :] = (G[yy(d), x, B, :].astype(f32) + Rbx[0, 1, yy(d)].astype(f32) + Rbx[1, 1, yy(d)].astype(f32)).astype(bf16)

    def qy1():
        for s in both:
            mail.send(f"qy1{s}", G.at[yy(4), x, hb2[s]], Rby.at[(1 - s) // 2, 0, hr[s]], ydev[s])

    def qy(hop):
        for s in both:
            i, yi = (1 - s) // 2, yy(s * (5 - hop))
            rows, inner = (hb2[s], hr[s]) if hop == 2 else (B, pl.ds(0, brows))
            mail.recv(f"qy{hop - 1}{s}", Rby.at[i, hop - 2, inner], ydev[s])
            G[yi, x, rows, :] = G[yi, x, rows, :] + Rby[i, hop - 2, inner, :]
            mail.send(f"qy{hop}{s}", G.at[yi, x, B], Rby.at[i, hop - 1], ydev[s])

    def qy_end():
        for s in both:
            mail.recv(f"qy4{s}", Rby.at[(1 - s) // 2, 3], ydev[s])
        finish(B, Rby[0, 3], Rby[1, 3])

    def dk_send(d):
        mail.send(f"dk{d}", D.at[zz(d), 1 - k], Rk.at[zz(d)], kdev)

    def dk_add(d):
        mail.recv(f"dk{d}", Rk.at[zz(d)], kdev)
        D[zz(d), k] = D[zz(d), k] + Rk[zz(d)]

    def dz1():
        dk_add(4)
        for s in both:
            mail.send(f"dz1{s}h{s}", D.at[zz(4), k, ht[s]], Rz.at[(1 - s) // 2, 0, ht[s]], zdev[s])

    def dz(hop):
        for s in both:
            i, d = (1 - s) // 2, s * (5 - hop)
            dk_add(d)
            zi = zz(d)
            for h in ((-s, s) if hop == 2 else (s, -s)):
                rows = ht[h]
                if hop > 2 or h == s:
                    mail.recv(f"dz{hop - 1}{s}h{h}", Rz.at[i, hop - 2, rows], zdev[s])
                    D[zi, k, rows, :] = D[zi, k, rows, :] + Rz[i, hop - 2, rows, :]
                mail.send(f"dz{hop}{s}h{h}", D.at[zi, k, rows], Rz.at[i, hop - 1, rows], zdev[s])

    def dz_end():
        dk_add(0)
        for h in both:
            for s in both:
                mail.recv(f"dz4{s}h{h}", Rz.at[(1 - s) // 2, 3, ht[h]], zdev[s])
            rows = ht[h]
            dx_out[rows, :] = (D[z, k, rows, :].astype(f32) + Rz[0, 3, rows, :].astype(f32) + Rz[1, 3, rows, :].astype(f32)).astype(bf16)

    def unpack():
        def piece(src, _):
            v = HR[src].astype(f32)
            upper = jnp.concatenate([v[:8, :768], v[8:, :768]], 1)
            lower = jnp.concatenate([v[4 * q:4 * q + 4, 768:] for q in range(4)], 1)
            hid_out[:, pl.ds(pl.multiple_of(src * 1536, 1536), 1536)] = jnp.concatenate([upper, lower], 0).astype(bf16)
            return 0

        lax.fori_loop(0, 16, piece, 0)

    send_hidden(4)

    def backward_round(r, _):
        terms(r)
        partial(r)

        @pl.when(r == 0)
        def _():
            qx1(4); dk_send(4); gy1(0); gy1(1)

        @pl.when(r == 1)
        def _():
            qx1(3); dk_send(3); dz1(); send_hidden(3, -3)

        @pl.when(r == 2)
        def _():
            qx1(-3); dk_send(-3)

        @pl.when(r == 3)
        def _():
            qx1(2); dk_send(2)

        @pl.when(r == 4)
        def _():
            qx2(4); qx1(-2); dk_send(-2); gy(2, 0); gy(2, 1)

        @pl.when(r == 5)
        def _():
            qx1(1); dk_send(1); dz(2); send_hidden(2, -2)

        @pl.when(r == 6)
        def _():
            qx2(3); qx2(-3); qx1(-1); dk_send(-1)

        @pl.when(r == 7)
        def _():
            qx1(0); dk_send(0)
        return 0

    lax.fori_loop(0, 8, backward_round, 0)
    qx_end(4); qy1()
    gy(3, 0); gy(3, 1)
    qx2(2); qx2(-2)
    dz(3); send_hidden(1, -1, 0)
    qx_end(3); qx_end(-3); qy(2)
    qx2(1); qx2(-1)
    gy(4, 0); gy(4, 1)
    qx_end(2); qx_end(-2); qy(3)
    qx2(0)
    dz(4)
    qx_end(1); qx_end(-1)
    gy_end(0); gy_end(1); gx1()
    qy(4)
    recv_hidden(4, 3, -3, 2, -2, 1, -1, 0)
    keep.wait()
    unpack()
    gx2()
    qx_end(0)
    dz_end()
    gx_end()
    mail.drain(like, kdev)
    qy_end()


def fused(slots, count, w, tokens, cot):
    vm = pl.BlockSpec(memory_space=pltpu.VMEM)
    sm = pl.BlockSpec(memory_space=pltpu.SMEM)
    hbm = pl.BlockSpec(memory_space=pl.ANY)
    V = pltpu.VMEM
    n = 256
    brows = 512 - acut
    return pl.pallas_call(
        kernel_body, name="block_sparse_ffn",
        out_shape=(
            jax.ShapeDtypeStruct((12, 24576), bf16),
            jax.ShapeDtypeStruct((192, 512), bf16),
            jax.ShapeDtypeStruct((512, 128), bf16),
        ),
        in_specs=[sm, sm, hbm, hbm, hbm], out_specs=(vm, vm, vm),
        scratch_shapes=[
            V((8, 4, wrows, 128), bf16), V((8, 2, 192, 512), bf16), V((192, 1536), f32),
            V((8, 4, 8, 128), jnp.int32), pltpu.SMEM((8, 4, 8, 128), jnp.int32),
            V((8, 1024, 1536), bf16), V((192, 1536), f32), V((12, 192, 128), bf16), V((192, 128), f32),
            V((16, 16, 1152), f32), V((16, 16, 1152), bf16), V((16, 16, 1152), bf16),
            V((8, 4, 512, 128), bf16), V((8, 2, 192, 512), bf16),
            V((2, 4, 4, acut, 128), bf16), V((2, 2, acut, 128), bf16),
            V((2, 2, 8, brows, 128), bf16), V((2, 4, brows, 128), bf16),
            V((8, 192, 512), bf16), V((2, 4, 192, 512), bf16),
            pltpu.SemaphoreType.DMA((n,)), pltpu.SemaphoreType.DMA((n,)),
            pltpu.SemaphoreType.DMA((4,)), pltpu.SemaphoreType.DMA((8,)),
        ],
        compiler_params=pltpu.CompilerParams(collective_id=0, has_side_effects=True, vmem_limit_bytes=62 * 2**20),
    )(slots, count, w, tokens, cot)


def body(tokens, weight_blocks, block_slots, block_counts, cotangent):
    hidden, dx, dw = fused(
        block_slots.reshape(4), block_counts.reshape(1), weight_blocks.reshape(512, 128), tokens, cotangent
    )
    return hidden, dx, dw.reshape(1, 1, 4, 128, 128)


def solution(mesh):
    in_specs = (
        P("row", "col"),
        P("row", "col", None, None, None),
        P("row", "col", None),
        P("row", "col"),
        P("row", "col"),
    )
    out_specs = (P(("row", "col"), None), P("row", "col"), P("row", "col", None, None, None))
    return jax.shard_map(body, mesh=mesh, in_specs=in_specs, out_specs=out_specs, check_vma=False)
```

```python
import functools
import math

import jax
import jax.numpy as jnp
from jax import lax
from jax.experimental import pallas as pl
from jax.experimental.pallas import tpu as pltpu
from jax.sharding import PartitionSpec as P

MESH = pl.DeviceIdType.MESH
ny, nx, nz, nk = 8, 4, 8, 2
both = (1, -1)
f32, bf16 = jnp.float32, jnp.bfloat16

gelu_scale = 0.7978845608028654
cubic_term = 0.044715

wrows = 528
wcut = 224
acut = 176


gather_order = [
    ("by0", 1), ("by0", -1), ("ax0", 1), ("tz0", 1), ("ax0", -1), ("ay0", 0), ("tz0", 2), ("tz0", 0), ("bxs", 0), ("tz0", 3), ("tz", 1, 1),
    ("ax", 1, -1), ("tk", 0), ("by", 1, 1), ("by", 1, -1), ("ax", 1, 1), ("bxs", 1), ("ays", 1), ("tz", 1, 2), ("ays", 2), ("bxs", -1), ("bx1", 0),
    ("tz", 1, 0), ("tz", 1, 3), ("tz", 2, 1), ("tk", 1), ("tk", -1), ("ax2",), ("ays", 3), ("by", 2, -1), ("by", 2, 1), ("bxs", 2), ("tz", 2, 0),
    ("ay", 1, 0), ("bx1", 1), ("tz", 2, 2), ("bx1", -1), ("bxs", -2), ("tz", 2, 3), ("ay", 1, 1), ("tz", 3, 1), ("tz", 3, 0), ("by", 3, -1),
    ("bxs", 3), ("tk", 2), ("bx2", 0), ("by", 3, 1), ("bxs", -3), ("bx2", -1), ("tz", 3, 3), ("tz", 3, 2), ("bx2", 1), ("codes", 2), ("ay", 2, 0),
    ("bx1", -2), ("tk", -3), ("codes", 0), ("tk", 3), ("tz", 4, 1), ("tk", -2), ("bx1", 2), ("tz", 4, 0), ("tk", 4), ("ay", 2, 1), ("bx1", 3),
    ("tk_end",), ("codes", 1), ("by4",), ("bxs", 4), ("apply", 0), ("apply", 1), ("apply", 2), ("bx1", -3), ("bx2", -2), ("ay", 3, 0), ("bx2", 2),
    ("codes", 3), ("apply", 3), ("codes", 4), ("bx2", 3), ("ay", 3, 1), ("bx1", 4), ("codes", 5), ("apply", 4), ("apply", 5), ("bx2", -3),
    ("codes", 6), ("apply", 6), ("bx2", 4), ("ay4",), ("codes", 7), ("apply", 7),
]
backward_order = [
    ("hid", 4), ("T", 0), ("qx1", 4), ("gy", 1, 1), ("P", 0), ("dks", 4), ("gy", 1, 0), ("T", 1), ("qx1", 3), ("P", 1), ("dz1",), ("T", 2),
    ("qx1", -3), ("P", 2), ("hid", -3), ("qx2", 4), ("gy", 2, 1), ("T", 3), ("dks", 3), ("dks", -3), ("hid", 1), ("qx1", 2), ("qx2", 3), ("P", 3),
    ("gy", 2, 0), ("dz", 2, 1), ("T", 4), ("qx2", -3), ("dz", 2, -1), ("qx_end", 4), ("qy", 1), ("qx1", -2), ("gy", 3, 1), ("P", 4), ("qx2", 2),
    ("hid", 2), ("T", 5), ("gy", 3, 0), ("qx1", 1), ("dks", 2), ("P", 5), ("T", 6), ("qx_end", 3), ("hid", -2), ("qx_end", -3), ("qy", 2), ("dks", 1),
    ("qx1", -1), ("dks", -2), ("dz", 3, 1), ("qx2", -2), ("gy", 4, 1), ("hid", 3), ("P", 6), ("T", 7), ("qx1", 0), ("dz", 3, -1), ("gy", 4, 0),
    ("qx2", 1), ("hid", -1), ("qx_end", 2), ("qx2", -1), ("qx_end", -2), ("dks", -1), ("qy", 3), ("P", 7), ("dz", 4, 1), ("gy_end", 1), ("gy_end", 0),
    ("gx1",), ("qx2", 0), ("dz", 4, -1), ("qx_end", 1), ("qx_end", -1), ("qy", 4), ("gx2",), ("hid", 0), ("dks", 0), ("qx_end", 0), ("fin",),
    ("qy_end",), ("gx_end",), ("dz_end",),
]


def gelu_pair(v):
    inner = gelu_scale * (v + cubic_term * v * v * v)
    th = jnp.tanh(inner)
    act = 0.5 * v * (1.0 + th)
    der = 0.5 * (1.0 + th) + 0.5 * v * (1.0 - th * th) * gelu_scale * (1.0 + 3.0 * cubic_term * v * v)
    return act, der


def wrap(v, n):
    return lax.rem(v + n, n)


def halves(start, rows):
    upper = (rows // 2 + 15) // 16 * 16
    return {1: pl.ds(start, upper), -1: pl.ds(start + upper, rows - upper)}


def split(order, marks):
    cuts = [-1] + [order.index(m) for m in marks] + [len(order)]
    return [order[a + 1:b] for a, b in zip(cuts, cuts[1:])]


def run(steps, part):
    for name, *args in part:
        steps[name](*args)


class Mail:
    def __init__(self, send_sem, recv_sem):
        self.send_sem, self.recv_sem = send_sem, recv_sem
        self.ids = {}
        self.sent = []

    def copy(self, name, src, dst, to):
        i = self.ids.setdefault(name, len(self.ids))
        return pltpu.make_async_remote_copy(
            src_ref=src, dst_ref=dst, send_sem=self.send_sem.at[i], recv_sem=self.recv_sem.at[i],
            device_id=to, device_id_type=MESH,
        )

    def send(self, name, src, dst, to):
        self.copy(name, src, dst, to).start()
        self.sent.append((name, tuple(src.shape)))

    def recv(self, name, dst, to):
        self.copy(name, dst, dst, to).wait_recv()

    def drain(self, like, to):
        for name, shape in self.sent:
            self.copy(name, like(shape), like(shape), to).wait_send()
        self.sent = []


def kernel_body(
    slot_ref, count_ref, w_ref, tok_ref, cot_ref,
    hid_out, dx_out, dw_out,
    W, T, cot, code_v, code, blocks, pre, gp, act_s, Hs, H, HR, G, D,
    Ray, Rax, Rbx, Rby, Rk, Rz,
    send_sem, recv_sem, own_sem, code_sem,
):
    r_me, c_me = lax.axis_index("row"), lax.axis_index("col")
    y, x, z, k = r_me // nx, lax.rem(r_me, nx), c_me // nk, lax.rem(c_me, nk)

    def device(yi, xi, zi, ki):
        return (yi * nx + xi, zi * nk + ki)

    own = [
        pltpu.make_async_copy(w_ref, W.at[y, x, pl.ds(0, 512)], own_sem.at[0]),
        pltpu.make_async_copy(tok_ref, T.at[z, k], own_sem.at[1]),
        pltpu.make_async_copy(cot_ref, cot, own_sem.at[2]),
    ]
    for c in own:
        c.start()

    yy = lambda d: wrap(y + d, ny)
    xx = lambda d: wrap(x + d, nx)
    zz = lambda d: wrap(z + d, nz)
    ydev = {s: device(yy(s), x, z, k) for s in both}
    xdev = {s: device(y, xx(s), z, k) for s in both}
    zdev = {s: device(y, x, zz(s), k) for s in both}
    kdev = device(y, x, z, 1 - k)

    bar = pltpu.get_barrier_semaphore()
    peers = [ydev[1], ydev[-1], xdev[1], xdev[-1]]
    peers += [device(y, x, zz(i), lax.rem(k + j, nk)) for i in range(nz) for j in range(nk) if i or j]
    for p in peers:
        pl.semaphore_signal(bar, inc=1, device_id=p, device_id_type=MESH)

    line = lax.broadcasted_iota(jnp.int32, (16, 128), 0)
    numbers = jnp.zeros((16, 128), f32)
    for s in range(4):
        number = jnp.where(s < count_ref[0], slot_ref[s], slot_ref[s] + 24)
        numbers = jnp.where(line == s, number.astype(f32), numbers)
    W[y, x, 512:528, :] = numbers.astype(bf16)
    pre[...] = jnp.zeros_like(pre)
    blocks[16] = jnp.zeros((128, 128), bf16)
    own[0].wait()
    own[1].wait()
    pl.semaphore_wait(bar, len(peers))

    mail = Mail(send_sem, recv_sem)

    def like(shape):
        if shape[-1] == 512:
            return T.at[0, 0, pl.ds(0, shape[0])]
        if shape[-1] == 1152:
            return H.at[0]
        if len(shape) == 3:
            return W.at[0, pl.ds(0, shape[0]), pl.ds(0, shape[1])]
        return W.at[0, 0, pl.ds(0, shape[0])]

    A = pl.ds(0, wcut)
    B = pl.ds(wcut, wrows - wcut)
    ha = halves(0, wcut)
    hb = halves(wcut, wrows - wcut)
    side = 1 - 2 * lax.rem(x, 2)
    pair = {0: pl.ds(2 * (x // 2), 2), 1: pl.ds(2 * (1 - x // 2), 2)}
    role_x = {0: x, 1: xx(side), 2: xx(-side), 3: xx(2)}
    chunk = {s: [pl.ds(48 * i, 48) for i in ((0, 1, 2, 3) if s == 1 else (2, 3, 0, 1))] for s in both}

    def by(hop, s):
        if hop == 0:
            mail.send(f"by1{s}", W.at[y, x, B], W.at[y, x, B], ydev[s])
            return
        piece = W.at[yy(-s * hop), x, B]
        mail.recv(f"by{hop}{s}", piece, ydev[s])
        if hop < 3:
            mail.send(f"by{hop + 1}{s}", piece, piece, ydev[s])
        else:
            half = W.at[yy(-s * hop), x, hb[s]]
            mail.send(f"by4{s}", half, half, ydev[s])

    def by4():
        for s in both:
            mail.recv(f"by4{s}", W.at[yy(4), x, hb[s]], ydev[s])

    def bxs(d):
        piece = W.at[yy(d), x, B]
        for t in both:
            mail.send(f"bx1{t}y{d}", piece, piece, xdev[t])

    def bx1(d):
        for t in both:
            mail.recv(f"bx1{t}y{d}", W.at[yy(d), xx(-t), B], xdev[t])
            half = W.at[yy(d), xx(-t), hb[t]]
            mail.send(f"bx2{t}y{d}", half, half, xdev[t])

    def bx2(d):
        for t in both:
            mail.recv(f"bx2{t}y{d}", W.at[yy(d), xx(2), hb[t]], xdev[t])

    def ax(hop, t):
        if hop == 0:
            mail.send(f"ax1{t}", W.at[y, x, A], W.at[y, x, A], xdev[t])
            return
        mail.recv(f"ax1{t}", W.at[y, xx(-t), A], xdev[t])
        half = W.at[y, xx(-t), ha[t]]
        mail.send(f"ax2{t}", half, half, xdev[t])

    def ax2():
        for t in both:
            mail.recv(f"ax2{t}", W.at[y, xx(2), ha[t]], xdev[t])

    def ays(role):
        piece = W.at[y, role_x[role], A]
        for s in both:
            mail.send(f"ay1{s}r{role}", piece, piece, ydev[s])

    def ay(hop, p):
        for s in both:
            piece = W.at[yy(-s * hop), pair[p], A]
            if hop == 1:
                for role in (2 * p, 2 * p + 1):
                    mail.recv(f"ay1{s}r{role}", W.at[yy(-s), role_x[role], A], ydev[s])
            else:
                mail.recv(f"ay{hop}{s}p{p}", piece, ydev[s])
            if hop < 3:
                mail.send(f"ay{hop + 1}{s}p{p}", piece, piece, ydev[s])
            else:
                half = W.at[yy(-s * hop), pair[p], ha[s]]
                mail.send(f"ay4{s}p{p}", half, half, ydev[s])

    def ay4():
        for p in range(2):
            for s in both:
                mail.recv(f"ay4{s}p{p}", W.at[yy(4), pair[p], ha[s]], ydev[s])

    def tz(hop, i):
        for s in both:
            piece = T.at[zz(-s * hop), k, chunk[s][i]]
            if 0 < hop < 4 or (hop == 4 and i < 2):
                mail.recv(f"tz{hop}{s}c{i}", piece, zdev[s])
            if hop < 3 or (hop == 3 and i < 2):
                mail.send(f"tz{hop + 1}{s}c{i}", piece, piece, zdev[s])

    def tk(d):
        mail.send(f"tk{d}", T.at[zz(d), k], T.at[zz(d), k], kdev)

    def tk_end():
        for d in (0, 1, -1, 2, -2, 3, -3, 4):
            mail.recv(f"tk{d}", T.at[zz(d), 1 - k], kdev)

    def near_first(r):
        m = (r + 1) // 2
        return m * (2 * lax.rem(r, 2) - 1)

    def codes(r):
        g = wrap(y + near_first(r), ny)
        for i in range(4):
            code_v[g, i] = W[g, i, 512:528, :][:8].astype(f32).astype(jnp.int32)
        pltpu.make_async_copy(code_v.at[g], code.at[g], code_sem.at[g]).start()

    def apply(r):
        g = wrap(y + near_first(r), ny)
        for i in range(4):
            for s in range(4):
                blocks[4 * i + s] = W[g, i, s * 128:(s + 1) * 128, :]
        pltpu.make_async_copy(code_v.at[g], code.at[g], code_sem.at[g]).wait()
        index = {}
        for i in range(4):
            n = [code[g, i, s, 0] for s in range(4)]
            for p in range(24):
                at = 16
                for s in (3, 2, 1, 0):
                    at = jnp.where(n[s] == p, 4 * i + s, at)
                index[i, p] = at
        for j in range(0, 12, 2):
            total = pre[:, j * 128:(j + 2) * 128]
            for h in range(2):
                rows = [
                    jnp.concatenate([blocks[index[i, 12 * u + j]], blocks[index[i, 12 * u + j + 1]]], 1)
                    for i in (2 * h, 2 * h + 1) for u in range(2)
                ]
                total = total + jnp.dot(T[g, h], jnp.concatenate(rows, 0), preferred_element_type=f32)
            pre[:, j * 128:(j + 2) * 128] = total

    steps = dict(by0=lambda s: by(0, s), by=by, by4=by4, bxs=bxs, bx1=bx1, bx2=bx2, ax0=lambda t: ax(0, t), ax=ax, ax2=ax2,
                 ay0=ays, ays=ays, ay=ay, ay4=ay4, tz0=lambda i: tz(0, i), tz=tz, tk=tk, tk_end=tk_end, codes=codes)
    parts = split(gather_order, [("apply", r) for r in range(8)])
    run(steps, parts[0])

    def gather_round(r, _):
        for i in range(1, 8):
            if parts[i]:
                pl.when(r == i)(functools.partial(run, steps, parts[i]))
        apply(r)
        return 0

    lax.fori_loop(0, 8, gather_round, 0)
    run(steps, parts[8])
    own[2].wait()

    def activation(i, _):
        for q in range(4):
            j = 3 * q + i
            cols = pl.ds(pl.multiple_of(j * 128, 128), 128)
            act, der = gelu_pair(pre[:, cols])
            gp[j] = (cot[:, cols] * der).astype(bf16)
            act_s[...] = act
            upper = pl.ds(pl.multiple_of((3 * (q % 2) + i) * 128, 128), 128)
            lower = pl.ds(pl.multiple_of(768 + i * 128, 128), 128)
            for c in range(16):
                Hs[c, 8 * (q // 2):8 * (q // 2) + 8, upper] = act_s[12 * c:12 * c + 8]
                Hs[c, 4 * q:4 * q + 4, lower] = act_s[12 * c + 8:12 * c + 12]
        return 0

    lax.fori_loop(0, 3, activation, 0)
    H[...] = Hs[...].astype(bf16)
    keep = pltpu.make_async_copy(H.at[c_me], HR.at[c_me], own_sem.at[3])
    keep.start()

    brows = 512 - acut
    A = pl.ds(0, acut)
    B = pl.ds(acut, brows)
    ha2 = halves(0, acut)
    hb2 = halves(acut, brows)
    hr = halves(0, brows)
    ht = {1: pl.ds(0, 96), -1: pl.ds(96, 96)}

    def far_first(r):
        m = (r + 1) // 2
        return (4 - m) * (2 * lax.rem(r, 2) - 1)

    def grad_cat(g, i):
        return jnp.concatenate([gp[jnp.clip(lax.rem(code[g, i, s, 0], 12), 0, 11)] for s in range(4)], 1)

    def terms(r):
        yi = wrap(y + far_first(r), ny)
        for i in range(4):
            tok = T[yi, i // 2, :, (i % 2) * 256:(i % 2 + 1) * 256]
            full = lax.dot_general(tok, grad_cat(yi, i), (((0,), (0,)), ((), ())), preferred_element_type=f32)
            for s in range(4):
                part = full[:, s * 128:(s + 1) * 128]
                G[yi, i, s * 128:(s + 1) * 128, :] = jnp.where(code[yi, i, s, 0] < 12, part[:128], part[128:]).astype(bf16)

    def partial(r):
        zi = wrap(z + far_first(r), nz)
        for i in range(4):
            top, bottom = [], []
            for s in range(4):
                w = W[zi, i, s * 128:(s + 1) * 128, :]
                n = code[zi, i, s, 0]
                top.append(jnp.where(n < 12, w, jnp.zeros_like(w)))
                bottom.append(jnp.where((n >= 12) & (n < 24), w, jnp.zeros_like(w)))
            wide = jnp.concatenate([jnp.concatenate(top, 1), jnp.concatenate(bottom, 1)], 0)
            out = lax.dot_general(grad_cat(zi, i), wide, (((1,), (1,)), ((), ())), preferred_element_type=f32)
            D[zi, i // 2, :, (i % 2) * 256:(i % 2 + 1) * 256] = out.astype(bf16)

    def send_hidden(*ds):
        for dz in ds:
            for dk in range(2):
                if dz or dk:
                    zi, ki = zz(dz), lax.rem(k + dk, 2)
                    mail.send(f"h{dz % 8}{dk}", H.at[zi * 2 + ki], HR.at[c_me], device(y, x, zi, ki))

    def recv_hidden(*ds):
        for dz in ds:
            for dk in range(2):
                if dz or dk:
                    mail.recv(f"h{dz % 8}{dk}", HR.at[zz(-dz) * 2 + lax.rem(k + dk, 2)], kdev)

    xpair = [pl.ds(0, 2), pl.ds(2, 2)]

    def gy1(p):
        for s in both:
            mail.send(f"gy1{s}p{p}", G.at[yy(4), xpair[p], ha2[s]], Ray.at[(1 - s) // 2, 0, xpair[p], ha2[s]], ydev[s])

    def gy(hop, p):
        for s in both:
            i, yi, xp = (1 - s) // 2, yy(s * (5 - hop)), xpair[p]
            rows = ha2[s] if hop == 2 else A
            mail.recv(f"gy{hop - 1}{s}p{p}", Ray.at[i, hop - 2, xp, rows], ydev[s])
            G[yi, xp, rows, :] = G[yi, xp, rows, :] + Ray[i, hop - 2, xp, rows, :]
            mail.send(f"gy{hop}{s}p{p}", G.at[yi, xp, A], Ray.at[i, hop - 1, xp, A], ydev[s])

    def gy_end(p):
        for s in both:
            mail.recv(f"gy4{s}p{p}", Ray.at[(1 - s) // 2, 3, xpair[p], A], ydev[s])
        xp = xpair[p]
        G[y, xp, A, :] = (G[y, xp, A, :].astype(f32) + Ray[0, 3, xp, A, :].astype(f32) + Ray[1, 3, xp, A, :].astype(f32)).astype(bf16)

    def gx1():
        for t in both:
            mail.send(f"gx1{t}", G.at[y, xx(2), ha2[t]], Rax.at[(1 - t) // 2, 0, ha2[t]], xdev[t])

    def gx2():
        for t in both:
            i = (1 - t) // 2
            mail.recv(f"gx1{t}", Rax.at[i, 0, ha2[t]], xdev[t])
            G[y, xx(t), ha2[t], :] = G[y, xx(t), ha2[t], :] + Rax[i, 0, ha2[t], :]
            mail.send(f"gx2{t}", G.at[y, xx(t), A], Rax.at[i, 1], xdev[t])

    def finish(rows, r0, r1):
        total = G[y, x, rows, :].astype(f32) + r0.astype(f32) + r1.astype(f32)
        row = lax.broadcasted_iota(jnp.int32, total.shape, 0) + rows.start
        usable = row < count_ref[0] * 128
        dw_out[rows, :] = jnp.where(usable, total * (1.0 / math.sqrt(6144)), 0.0).astype(bf16)

    def gx_end():
        for t in both:
            mail.recv(f"gx2{t}", Rax.at[(1 - t) // 2, 1], xdev[t])
        finish(A, Rax[0, 1], Rax[1, 1])

    def qx1(d):
        for t in both:
            mail.send(f"qx1{t}y{d}", G.at[yy(d), xx(2), hb2[t]], Rbx.at[(1 - t) // 2, 0, yy(d), hr[t]], xdev[t])

    def qx2(d):
        for t in both:
            i = (1 - t) // 2
            mail.recv(f"qx1{t}y{d}", Rbx.at[i, 0, yy(d), hr[t]], xdev[t])
            G[yy(d), xx(t), hb2[t], :] = G[yy(d), xx(t), hb2[t], :] + Rbx[i, 0, yy(d), hr[t], :]
            mail.send(f"qx2{t}y{d}", G.at[yy(d), xx(t), B], Rbx.at[i, 1, yy(d)], xdev[t])

    def qx_end(d):
        for t in both:
            mail.recv(f"qx2{t}y{d}", Rbx.at[(1 - t) // 2, 1, yy(d)], xdev[t])
        G[yy(d), x, B, :] = (G[yy(d), x, B, :].astype(f32) + Rbx[0, 1, yy(d)].astype(f32) + Rbx[1, 1, yy(d)].astype(f32)).astype(bf16)

    def qy1():
        for s in both:
            mail.send(f"qy1{s}", G.at[yy(4), x, hb2[s]], Rby.at[(1 - s) // 2, 0, hr[s]], ydev[s])

    def qy(hop):
        for s in both:
            i, yi = (1 - s) // 2, yy(s * (5 - hop))
            rows, inner = (hb2[s], hr[s]) if hop == 2 else (B, pl.ds(0, brows))
            mail.recv(f"qy{hop - 1}{s}", Rby.at[i, hop - 2, inner], ydev[s])
            G[yi, x, rows, :] = G[yi, x, rows, :] + Rby[i, hop - 2, inner, :]
            mail.send(f"qy{hop}{s}", G.at[yi, x, B], Rby.at[i, hop - 1], ydev[s])

    def qy_end():
        for s in both:
            mail.recv(f"qy4{s}", Rby.at[(1 - s) // 2, 3], ydev[s])
        finish(B, Rby[0, 3], Rby[1, 3])

    def dk_send(d):
        mail.send(f"dk{d}", D.at[zz(d), 1 - k], Rk.at[zz(d)], kdev)

    def dk_add(d):
        mail.recv(f"dk{d}", Rk.at[zz(d)], kdev)
        D[zz(d), k] = D[zz(d), k] + Rk[zz(d)]

    def dz1():
        dk_add(4)
        for s in both:
            mail.send(f"dz1{s}h{s}", D.at[zz(4), k, ht[s]], Rz.at[(1 - s) // 2, 0, ht[s]], zdev[s])

    def dz(hop, s):
        i, d = (1 - s) // 2, s * (5 - hop)
        dk_add(d)
        zi = zz(d)
        for h in ((-s, s) if hop == 2 else (s, -s)):
            rows = ht[h]
            if hop > 2 or h == s:
                mail.recv(f"dz{hop - 1}{s}h{h}", Rz.at[i, hop - 2, rows], zdev[s])
                D[zi, k, rows, :] = D[zi, k, rows, :] + Rz[i, hop - 2, rows, :]
            mail.send(f"dz{hop}{s}h{h}", D.at[zi, k, rows], Rz.at[i, hop - 1, rows], zdev[s])

    def dz_end():
        dk_add(0)
        for h in both:
            for s in both:
                mail.recv(f"dz4{s}h{h}", Rz.at[(1 - s) // 2, 3, ht[h]], zdev[s])
            rows = ht[h]
            dx_out[rows, :] = (D[z, k, rows, :].astype(f32) + Rz[0, 3, rows, :].astype(f32) + Rz[1, 3, rows, :].astype(f32)).astype(bf16)

    def unpack():
        def piece(src, _):
            v = HR[src].astype(f32)
            upper = jnp.concatenate([v[:8, :768], v[8:, :768]], 1)
            lower = jnp.concatenate([v[4 * q:4 * q + 4, 768:] for q in range(4)], 1)
            hid_out[:, pl.ds(pl.multiple_of(src * 1536, 1536), 1536)] = jnp.concatenate([upper, lower], 0).astype(bf16)
            return 0

        lax.fori_loop(0, 16, piece, 0)

    def finish_hidden():
        recv_hidden(4, 3, -3, 2, -2, 1, -1, 0)
        keep.wait()
        unpack()

    steps = dict(hid=send_hidden, qx1=qx1, qx2=qx2, qx_end=qx_end, qy=lambda hop: qy(hop) if hop > 1 else qy1(), qy_end=qy_end,
                 gy=lambda hop, p: gy(hop, p) if hop > 1 else gy1(p), gy_end=gy_end, gx1=gx1, gx2=gx2, gx_end=gx_end,
                 dks=dk_send, dz1=dz1, dz=dz, dz_end=dz_end, fin=finish_hidden)
    parts2 = split(backward_order, [(u, r) for r in range(8) for u in ("T", "P")])

    def backward_round(r, _):
        for work, offset in ((terms, 0), (partial, 1)):
            for i in range(8):
                if parts2[2 * i + offset]:
                    pl.when(r == i)(functools.partial(run, steps, parts2[2 * i + offset]))
            work(r)
        return 0

    lax.fori_loop(0, 8, backward_round, 0)
    run(steps, parts2[16])
    mail.drain(like, kdev)


def fused(slots, count, w, tokens, cot):
    vm = pl.BlockSpec(memory_space=pltpu.VMEM)
    sm = pl.BlockSpec(memory_space=pltpu.SMEM)
    hbm = pl.BlockSpec(memory_space=pl.ANY)
    V = pltpu.VMEM
    n = 256
    brows = 512 - acut
    return pl.pallas_call(
        kernel_body, name="block_sparse_ffn",
        out_shape=(
            jax.ShapeDtypeStruct((12, 24576), bf16),
            jax.ShapeDtypeStruct((192, 512), bf16),
            jax.ShapeDtypeStruct((512, 128), bf16),
        ),
        in_specs=[sm, sm, hbm, hbm, hbm], out_specs=(vm, vm, vm),
        scratch_shapes=[
            V((8, 4, wrows, 128), bf16), V((8, 2, 192, 512), bf16), V((192, 1536), f32),
            V((8, 4, 8, 128), jnp.int32), pltpu.SMEM((8, 4, 8, 128), jnp.int32),
            V((17, 128, 128), bf16), V((192, 1536), f32), V((12, 192, 128), bf16), V((192, 128), f32),
            V((16, 16, 1152), f32), V((16, 16, 1152), bf16), V((16, 16, 1152), bf16),
            V((8, 4, 512, 128), bf16), V((8, 2, 192, 512), bf16),
            V((2, 4, 4, acut, 128), bf16), V((2, 2, acut, 128), bf16),
            V((2, 2, 8, brows, 128), bf16), V((2, 4, brows, 128), bf16),
            V((8, 192, 512), bf16), V((2, 4, 192, 512), bf16),
            pltpu.SemaphoreType.DMA((n,)), pltpu.SemaphoreType.DMA((n,)),
            pltpu.SemaphoreType.DMA((4,)), pltpu.SemaphoreType.DMA((8,)),
        ],
        compiler_params=pltpu.CompilerParams(collective_id=0, has_side_effects=True, vmem_limit_bytes=62 * 2**20),
    )(slots, count, w, tokens, cot)


def body(tokens, weight_blocks, block_slots, block_counts, cotangent):
    hidden, dx, dw = fused(
        block_slots.reshape(4), block_counts.reshape(1), weight_blocks.reshape(512, 128), tokens, cotangent
    )
    return hidden, dx, dw.reshape(1, 1, 4, 128, 128)


def solution(mesh):
    in_specs = (
        P("row", "col"),
        P("row", "col", None, None, None),
        P("row", "col", None),
        P("row", "col"),
        P("row", "col"),
    )
    out_specs = (P(("row", "col"), None), P("row", "col"), P("row", "col", None, None, None))
    return jax.shard_map(body, mesh=mesh, in_specs=in_specs, out_specs=out_specs, check_vma=False)
```

```python
import functools
import math

import jax
import jax.numpy as jnp
from jax import lax
from jax.experimental import pallas as pl
from jax.experimental.pallas import tpu as pltpu
from jax.sharding import PartitionSpec as P

MESH = pl.DeviceIdType.MESH
ny, nx, nz, nk = 8, 4, 8, 2
both = (1, -1)
f32, bf16 = jnp.float32, jnp.bfloat16

gelu_scale = 0.7978845608028654
cubic_term = 0.044715

wrows = 528
wcut = 224
acut = 176


gather_order = [
    ("by0", 1), ("by0", -1), ("ax0", 1), ("tz0", 1), ("ax0", -1), ("ay0", 0), ("tz0", 2), ("tz0", 0), ("bxs", 0), ("tz0", 3), ("tz", 1, 1),
    ("ax", 1, -1), ("tk", 0), ("by", 1, 1), ("by", 1, -1), ("ax", 1, 1), ("bxs", 1), ("ays", 1), ("tz", 1, 2), ("ays", 2), ("bxs", -1), ("bx1", 0),
    ("tz", 1, 0), ("tz", 1, 3), ("tz", 2, 1), ("tk", 1), ("tk", -1), ("ax2",), ("ays", 3), ("by", 2, -1), ("by", 2, 1), ("bxs", 2), ("tz", 2, 0),
    ("ay", 1, 0), ("bx1", 1), ("tz", 2, 2), ("bx1", -1), ("bxs", -2), ("tz", 2, 3), ("ay", 1, 1), ("tz", 3, 1), ("tz", 3, 0), ("by", 3, -1),
    ("bxs", 3), ("tk", 2), ("bx2", 0), ("by", 3, 1), ("bxs", -3), ("bx2", -1), ("tz", 3, 3), ("tz", 3, 2), ("bx2", 1), ("codes", 2), ("ay", 2, 0),
    ("bx1", -2), ("tk", -3), ("codes", 0), ("tk", 3), ("tz", 4, 1), ("tk", -2), ("bx1", 2), ("tz", 4, 0), ("tk", 4), ("ay", 2, 1), ("bx1", 3),
    ("tk_end",), ("codes", 1), ("by4",), ("bxs", 4), ("apply", 0), ("apply", 1), ("apply", 2), ("bx1", -3), ("bx2", -2), ("ay", 3, 0), ("bx2", 2),
    ("codes", 3), ("apply", 3), ("codes", 4), ("bx2", 3), ("ay", 3, 1), ("bx1", 4), ("codes", 5), ("apply", 4), ("apply", 5), ("bx2", -3),
    ("codes", 6), ("apply", 6), ("bx2", 4), ("ay4",), ("codes", 7), ("apply", 7),
]
backward_order = [
    ("hid", 4), ("T", 0), ("qx1", 4), ("gy", 1, 1), ("P", 0), ("dks", 4), ("gy", 1, 0), ("T", 1), ("qx1", 3), ("P", 1), ("dz1",), ("T", 2),
    ("qx1", -3), ("P", 2), ("hid", -3), ("qx2", 4), ("gy", 2, 1), ("T", 3), ("dks", 3), ("dks", -3), ("hid", 1), ("qx1", 2), ("qx2", 3), ("P", 3),
    ("gy", 2, 0), ("dz", 2, 1), ("T", 4), ("qx2", -3), ("dz", 2, -1), ("qx_end", 4), ("qy", 1), ("qx1", -2), ("gy", 3, 1), ("P", 4), ("qx2", 2),
    ("hid", 2), ("T", 5), ("gy", 3, 0), ("qx1", 1), ("dks", 2), ("P", 5), ("T", 6), ("qx_end", 3), ("hid", -2), ("qx_end", -3), ("qy", 2), ("dks", 1),
    ("qx1", -1), ("dks", -2), ("dz", 3, 1), ("qx2", -2), ("gy", 4, 1), ("hid", 3), ("P", 6), ("T", 7), ("qx1", 0), ("dz", 3, -1), ("gy", 4, 0),
    ("qx2", 1), ("hid", -1), ("qx_end", 2), ("qx2", -1), ("qx_end", -2), ("dks", -1), ("qy", 3), ("P", 7), ("dz", 4, 1), ("gy_end", 1), ("gy_end", 0),
    ("gx1",), ("drain",), ("qx2", 0), ("dz", 4, -1), ("qx_end", 1), ("qx_end", -1), ("qy", 4), ("gx2",), ("hid", 0), ("dks", 0), ("qx_end", 0),
    ("fin",), ("qy_end",), ("gx_end",), ("dz_end",),
]


def gelu_pair(v):
    inner = gelu_scale * (v + cubic_term * v * v * v)
    th = jnp.tanh(inner)
    act = 0.5 * v * (1.0 + th)
    der = 0.5 * (1.0 + th) + 0.5 * v * (1.0 - th * th) * gelu_scale * (1.0 + 3.0 * cubic_term * v * v)
    return act, der


def wrap(v, n):
    return lax.rem(v + n, n)


def halves(start, rows):
    upper = (rows // 2 + 15) // 16 * 16
    return {1: pl.ds(start, upper), -1: pl.ds(start + upper, rows - upper)}


def split(order, marks):
    cuts = [-1] + [order.index(m) for m in marks] + [len(order)]
    return [order[a + 1:b] for a, b in zip(cuts, cuts[1:])]


def run(steps, part):
    for name, *args in part:
        steps[name](*args)


class Mail:
    def __init__(self, send_sem, recv_sem):
        self.send_sem, self.recv_sem = send_sem, recv_sem
        self.ids = {}
        self.sent = []

    def copy(self, name, src, dst, to):
        i = self.ids.setdefault(name, len(self.ids))
        return pltpu.make_async_remote_copy(
            src_ref=src, dst_ref=dst, send_sem=self.send_sem.at[i], recv_sem=self.recv_sem.at[i],
            device_id=to, device_id_type=MESH,
        )

    def send(self, name, src, dst, to):
        self.copy(name, src, dst, to).start()
        self.sent.append((name, tuple(src.shape)))

    def recv(self, name, dst, to):
        self.copy(name, dst, dst, to).wait_recv()

    def drain(self, like, to, sent):
        for name, shape in sent:
            self.copy(name, like(shape), like(shape), to).wait_send()


def kernel_body(
    slot_ref, count_ref, w_ref, tok_ref, cot_ref,
    hid_out, dx_out, dw_out,
    W, T, cot, code_v, code, blocks, pre, gp, act_s, Hs, H, HR, G, D,
    Ray, Rax, Rbx, Rby, Rk, Rz,
    send_sem, recv_sem, own_sem, code_sem,
):
    r_me, c_me = lax.axis_index("row"), lax.axis_index("col")
    y, x, z, k = r_me // nx, lax.rem(r_me, nx), c_me // nk, lax.rem(c_me, nk)

    def device(yi, xi, zi, ki):
        return (yi * nx + xi, zi * nk + ki)

    own = [
        pltpu.make_async_copy(w_ref, W.at[y, x, pl.ds(0, 512)], own_sem.at[0]),
        pltpu.make_async_copy(tok_ref, T.at[z, k], own_sem.at[1]),
        pltpu.make_async_copy(cot_ref, cot, own_sem.at[2]),
    ]
    for c in own:
        c.start()

    yy = lambda d: wrap(y + d, ny)
    xx = lambda d: wrap(x + d, nx)
    zz = lambda d: wrap(z + d, nz)
    ydev = {s: device(yy(s), x, z, k) for s in both}
    xdev = {s: device(y, xx(s), z, k) for s in both}
    zdev = {s: device(y, x, zz(s), k) for s in both}
    kdev = device(y, x, z, 1 - k)

    bar = pltpu.get_barrier_semaphore()
    peers = [ydev[1], ydev[-1], xdev[1], xdev[-1], zdev[1], zdev[-1], kdev]
    for p in peers:
        pl.semaphore_signal(bar, inc=1, device_id=p, device_id_type=MESH)

    line = lax.broadcasted_iota(jnp.int32, (16, 128), 0)
    numbers = jnp.zeros((16, 128), f32)
    for s in range(4):
        number = jnp.where(s < count_ref[0], slot_ref[s], slot_ref[s] + 24)
        numbers = jnp.where(line == s, number.astype(f32), numbers)
    W[y, x, 512:528, :] = numbers.astype(bf16)
    pre[...] = jnp.zeros_like(pre)
    blocks[16] = jnp.zeros((128, 128), bf16)
    own[0].wait()
    own[1].wait()
    pl.semaphore_wait(bar, len(peers))

    mail = Mail(send_sem, recv_sem)

    def like(shape):
        if shape[-1] == 512:
            return T.at[0, 0, pl.ds(0, shape[0])]
        if shape[-1] == 1152:
            return H.at[0]
        if len(shape) == 3:
            return W.at[0, pl.ds(0, shape[0]), pl.ds(0, shape[1])]
        return W.at[0, 0, pl.ds(0, shape[0])]

    A = pl.ds(0, wcut)
    B = pl.ds(wcut, wrows - wcut)
    ha = halves(0, wcut)
    hb = halves(wcut, wrows - wcut)
    side = 1 - 2 * lax.rem(x, 2)
    pair = {0: pl.ds(2 * (x // 2), 2), 1: pl.ds(2 * (1 - x // 2), 2)}
    role_x = {0: x, 1: xx(side), 2: xx(-side), 3: xx(2)}
    chunk = {s: [pl.ds(48 * i, 48) for i in ((0, 1, 2, 3) if s == 1 else (2, 3, 0, 1))] for s in both}

    def by(hop, s):
        if hop == 0:
            mail.send(f"by1{s}", W.at[y, x, B], W.at[y, x, B], ydev[s])
            return
        piece = W.at[yy(-s * hop), x, B]
        mail.recv(f"by{hop}{s}", piece, ydev[s])
        if hop < 3:
            mail.send(f"by{hop + 1}{s}", piece, piece, ydev[s])
        else:
            half = W.at[yy(-s * hop), x, hb[s]]
            mail.send(f"by4{s}", half, half, ydev[s])

    def by4():
        for s in both:
            mail.recv(f"by4{s}", W.at[yy(4), x, hb[s]], ydev[s])

    def bxs(d):
        piece = W.at[yy(d), x, B]
        for t in both:
            mail.send(f"bx1{t}y{d}", piece, piece, xdev[t])

    def bx1(d):
        for t in both:
            mail.recv(f"bx1{t}y{d}", W.at[yy(d), xx(-t), B], xdev[t])
            half = W.at[yy(d), xx(-t), hb[t]]
            mail.send(f"bx2{t}y{d}", half, half, xdev[t])

    def bx2(d):
        for t in both:
            mail.recv(f"bx2{t}y{d}", W.at[yy(d), xx(2), hb[t]], xdev[t])

    def ax(hop, t):
        if hop == 0:
            mail.send(f"ax1{t}", W.at[y, x, A], W.at[y, x, A], xdev[t])
            return
        mail.recv(f"ax1{t}", W.at[y, xx(-t), A], xdev[t])
        half = W.at[y, xx(-t), ha[t]]
        mail.send(f"ax2{t}", half, half, xdev[t])

    def ax2():
        for t in both:
            mail.recv(f"ax2{t}", W.at[y, xx(2), ha[t]], xdev[t])

    def ays(role):
        piece = W.at[y, role_x[role], A]
        for s in both:
            mail.send(f"ay1{s}r{role}", piece, piece, ydev[s])

    def ay(hop, p):
        for s in both:
            piece = W.at[yy(-s * hop), pair[p], A]
            if hop == 1:
                for role in (2 * p, 2 * p + 1):
                    mail.recv(f"ay1{s}r{role}", W.at[yy(-s), role_x[role], A], ydev[s])
            else:
                mail.recv(f"ay{hop}{s}p{p}", piece, ydev[s])
            if hop < 3:
                mail.send(f"ay{hop + 1}{s}p{p}", piece, piece, ydev[s])
            else:
                half = W.at[yy(-s * hop), pair[p], ha[s]]
                mail.send(f"ay4{s}p{p}", half, half, ydev[s])

    def ay4():
        for p in range(2):
            for s in both:
                mail.recv(f"ay4{s}p{p}", W.at[yy(4), pair[p], ha[s]], ydev[s])

    def tz(hop, i):
        for s in both:
            piece = T.at[zz(-s * hop), k, chunk[s][i]]
            if 0 < hop < 4 or (hop == 4 and i < 2):
                mail.recv(f"tz{hop}{s}c{i}", piece, zdev[s])
            if hop < 3 or (hop == 3 and i < 2):
                mail.send(f"tz{hop + 1}{s}c{i}", piece, piece, zdev[s])

    def tk(d):
        mail.send(f"tk{d}", T.at[zz(d), k], T.at[zz(d), k], kdev)

    def tk_end():
        for d in (0, 1, -1, 2, -2, 3, -3, 4):
            mail.recv(f"tk{d}", T.at[zz(d), 1 - k], kdev)

    def near_first(r):
        m = (r + 1) // 2
        return m * (2 * lax.rem(r, 2) - 1)

    def codes(r):
        g = wrap(y + near_first(r), ny)
        for i in range(4):
            code_v[g, i] = W[g, i, 512:528, :][:8].astype(f32).astype(jnp.int32)
        pltpu.make_async_copy(code_v.at[g], code.at[g], code_sem.at[g]).start()

    def apply(r):
        g = wrap(y + near_first(r), ny)
        for i in range(4):
            for s in range(4):
                blocks[4 * i + s] = W[g, i, s * 128:(s + 1) * 128, :]
        pltpu.make_async_copy(code_v.at[g], code.at[g], code_sem.at[g]).wait()
        index = {}
        for i in range(4):
            n = [code[g, i, s, 0] for s in range(4)]
            for p in range(24):
                at = 16
                for s in (3, 2, 1, 0):
                    at = jnp.where(n[s] == p, 4 * i + s, at)
                index[i, p] = at
        for j in range(0, 12, 2):
            total = pre[:, j * 128:(j + 2) * 128]
            for h in range(2):
                rows = [
                    jnp.concatenate([blocks[index[i, 12 * u + j]], blocks[index[i, 12 * u + j + 1]]], 1)
                    for i in (2 * h, 2 * h + 1) for u in range(2)
                ]
                total = total + jnp.dot(T[g, h], jnp.concatenate(rows, 0), preferred_element_type=f32)
            pre[:, j * 128:(j + 2) * 128] = total

    steps = dict(by0=lambda s: by(0, s), by=by, by4=by4, bxs=bxs, bx1=bx1, bx2=bx2, ax0=lambda t: ax(0, t), ax=ax, ax2=ax2,
                 ay0=ays, ays=ays, ay=ay, ay4=ay4, tz0=lambda i: tz(0, i), tz=tz, tk=tk, tk_end=tk_end, codes=codes)
    parts = split(gather_order, [("apply", r) for r in range(8)])
    run(steps, parts[0])

    def gather_round(r, _):
        for i in range(1, 8):
            if parts[i]:
                pl.when(r == i)(functools.partial(run, steps, parts[i]))
        apply(r)
        return 0

    lax.fori_loop(0, 8, gather_round, 0)
    run(steps, parts[8])
    own[2].wait()

    def activation(i, _):
        for q in range(4):
            j = 3 * q + i
            cols = pl.ds(pl.multiple_of(j * 128, 128), 128)
            act, der = gelu_pair(pre[:, cols])
            gp[j] = (cot[:, cols] * der).astype(bf16)
            act_s[...] = act
            upper = pl.ds(pl.multiple_of((3 * (q % 2) + i) * 128, 128), 128)
            lower = pl.ds(pl.multiple_of(768 + i * 128, 128), 128)
            for c in range(16):
                Hs[c, 8 * (q // 2):8 * (q // 2) + 8, upper] = act_s[12 * c:12 * c + 8]
                Hs[c, 4 * q:4 * q + 4, lower] = act_s[12 * c + 8:12 * c + 12]
        return 0

    lax.fori_loop(0, 3, activation, 0)
    H[...] = Hs[...].astype(bf16)
    keep = pltpu.make_async_copy(H.at[c_me], HR.at[c_me], own_sem.at[3])
    keep.start()

    brows = 512 - acut
    A = pl.ds(0, acut)
    B = pl.ds(acut, brows)
    ha2 = halves(0, acut)
    hb2 = halves(acut, brows)
    hr = halves(0, brows)
    ht = {1: pl.ds(0, 96), -1: pl.ds(96, 96)}

    def far_first(r):
        m = (r + 1) // 2
        return (4 - m) * (2 * lax.rem(r, 2) - 1)

    def grad_cat(g, i):
        return jnp.concatenate([gp[jnp.clip(lax.rem(code[g, i, s, 0], 12), 0, 11)] for s in range(4)], 1)

    def terms(r):
        yi = wrap(y + far_first(r), ny)
        for i in range(4):
            tok = T[yi, i // 2, :, (i % 2) * 256:(i % 2 + 1) * 256]
            full = lax.dot_general(tok, grad_cat(yi, i), (((0,), (0,)), ((), ())), preferred_element_type=f32)
            for s in range(4):
                part = full[:, s * 128:(s + 1) * 128]
                G[yi, i, s * 128:(s + 1) * 128, :] = jnp.where(code[yi, i, s, 0] < 12, part[:128], part[128:]).astype(bf16)

    def partial(r):
        zi = wrap(z + far_first(r), nz)
        for i in range(4):
            top, bottom = [], []
            for s in range(4):
                w = W[zi, i, s * 128:(s + 1) * 128, :]
                n = code[zi, i, s, 0]
                top.append(jnp.where(n < 12, w, jnp.zeros_like(w)))
                bottom.append(jnp.where((n >= 12) & (n < 24), w, jnp.zeros_like(w)))
            wide = jnp.concatenate([jnp.concatenate(top, 1), jnp.concatenate(bottom, 1)], 0)
            out = lax.dot_general(grad_cat(zi, i), wide, (((1,), (1,)), ((), ())), preferred_element_type=f32)
            D[zi, i // 2, :, (i % 2) * 256:(i % 2 + 1) * 256] = out.astype(bf16)

    def send_hidden(*ds):
        for dz in ds:
            for dk in range(2):
                if dz or dk:
                    zi, ki = zz(dz), lax.rem(k + dk, 2)
                    mail.send(f"h{dz % 8}{dk}", H.at[zi * 2 + ki], HR.at[c_me], device(y, x, zi, ki))

    def recv_hidden(*ds):
        for dz in ds:
            for dk in range(2):
                if dz or dk:
                    mail.recv(f"h{dz % 8}{dk}", HR.at[zz(-dz) * 2 + lax.rem(k + dk, 2)], kdev)

    xpair = [pl.ds(0, 2), pl.ds(2, 2)]

    def gy1(p):
        for s in both:
            mail.send(f"gy1{s}p{p}", G.at[yy(4), xpair[p], ha2[s]], Ray.at[(1 - s) // 2, 0, xpair[p], ha2[s]], ydev[s])

    def gy(hop, p):
        for s in both:
            i, yi, xp = (1 - s) // 2, yy(s * (5 - hop)), xpair[p]
            rows = ha2[s] if hop == 2 else A
            mail.recv(f"gy{hop - 1}{s}p{p}", Ray.at[i, hop - 2, xp, rows], ydev[s])
            G[yi, xp, rows, :] = G[yi, xp, rows, :] + Ray[i, hop - 2, xp, rows, :]
            mail.send(f"gy{hop}{s}p{p}", G.at[yi, xp, A], Ray.at[i, hop - 1, xp, A], ydev[s])

    def gy_end(p):
        for s in both:
            mail.recv(f"gy4{s}p{p}", Ray.at[(1 - s) // 2, 3, xpair[p], A], ydev[s])
        xp = xpair[p]
        G[y, xp, A, :] = (G[y, xp, A, :].astype(f32) + Ray[0, 3, xp, A, :].astype(f32) + Ray[1, 3, xp, A, :].astype(f32)).astype(bf16)

    def gx1():
        for t in both:
            mail.send(f"gx1{t}", G.at[y, xx(2), ha2[t]], Rax.at[(1 - t) // 2, 0, ha2[t]], xdev[t])

    def gx2():
        for t in both:
            i = (1 - t) // 2
            mail.recv(f"gx1{t}", Rax.at[i, 0, ha2[t]], xdev[t])
            G[y, xx(t), ha2[t], :] = G[y, xx(t), ha2[t], :] + Rax[i, 0, ha2[t], :]
            mail.send(f"gx2{t}", G.at[y, xx(t), A], Rax.at[i, 1], xdev[t])

    def finish(rows, r0, r1):
        total = G[y, x, rows, :].astype(f32) + r0.astype(f32) + r1.astype(f32)
        row = lax.broadcasted_iota(jnp.int32, total.shape, 0) + rows.start
        usable = row < count_ref[0] * 128
        dw_out[rows, :] = jnp.where(usable, total * (1.0 / math.sqrt(6144)), 0.0).astype(bf16)

    def gx_end():
        for t in both:
            mail.recv(f"gx2{t}", Rax.at[(1 - t) // 2, 1], xdev[t])
        finish(A, Rax[0, 1], Rax[1, 1])

    def qx1(d):
        for t in both:
            mail.send(f"qx1{t}y{d}", G.at[yy(d), xx(2), hb2[t]], Rbx.at[(1 - t) // 2, 0, yy(d), hr[t]], xdev[t])

    def qx2(d):
        for t in both:
            i = (1 - t) // 2
            mail.recv(f"qx1{t}y{d}", Rbx.at[i, 0, yy(d), hr[t]], xdev[t])
            G[yy(d), xx(t), hb2[t], :] = G[yy(d), xx(t), hb2[t], :] + Rbx[i, 0, yy(d), hr[t], :]
            mail.send(f"qx2{t}y{d}", G.at[yy(d), xx(t), B], Rbx.at[i, 1, yy(d)], xdev[t])

    def qx_end(d):
        for t in both:
            mail.recv(f"qx2{t}y{d}", Rbx.at[(1 - t) // 2, 1, yy(d)], xdev[t])
        G[yy(d), x, B, :] = (G[yy(d), x, B, :].astype(f32) + Rbx[0, 1, yy(d)].astype(f32) + Rbx[1, 1, yy(d)].astype(f32)).astype(bf16)

    def qy1():
        for s in both:
            mail.send(f"qy1{s}", G.at[yy(4), x, hb2[s]], Rby.at[(1 - s) // 2, 0, hr[s]], ydev[s])

    def qy(hop):
        for s in both:
            i, yi = (1 - s) // 2, yy(s * (5 - hop))
            rows, inner = (hb2[s], hr[s]) if hop == 2 else (B, pl.ds(0, brows))
            mail.recv(f"qy{hop - 1}{s}", Rby.at[i, hop - 2, inner], ydev[s])
            G[yi, x, rows, :] = G[yi, x, rows, :] + Rby[i, hop - 2, inner, :]
            mail.send(f"qy{hop}{s}", G.at[yi, x, B], Rby.at[i, hop - 1], ydev[s])

    def qy_end():
        for s in both:
            mail.recv(f"qy4{s}", Rby.at[(1 - s) // 2, 3], ydev[s])
        finish(B, Rby[0, 3], Rby[1, 3])

    def dk_send(d):
        mail.send(f"dk{d}", D.at[zz(d), 1 - k], Rk.at[zz(d)], kdev)

    def dk_add(d):
        mail.recv(f"dk{d}", Rk.at[zz(d)], kdev)
        D[zz(d), k] = D[zz(d), k] + Rk[zz(d)]

    def dz1():
        dk_add(4)
        for s in both:
            mail.send(f"dz1{s}h{s}", D.at[zz(4), k, ht[s]], Rz.at[(1 - s) // 2, 0, ht[s]], zdev[s])

    def dz(hop, s):
        i, d = (1 - s) // 2, s * (5 - hop)
        dk_add(d)
        zi = zz(d)
        for h in ((-s, s) if hop == 2 else (s, -s)):
            rows = ht[h]
            if hop > 2 or h == s:
                mail.recv(f"dz{hop - 1}{s}h{h}", Rz.at[i, hop - 2, rows], zdev[s])
                D[zi, k, rows, :] = D[zi, k, rows, :] + Rz[i, hop - 2, rows, :]
            mail.send(f"dz{hop}{s}h{h}", D.at[zi, k, rows], Rz.at[i, hop - 1, rows], zdev[s])

    def dz_end():
        dk_add(0)
        for h in both:
            for s in both:
                mail.recv(f"dz4{s}h{h}", Rz.at[(1 - s) // 2, 3, ht[h]], zdev[s])
            rows = ht[h]
            dx_out[rows, :] = (D[z, k, rows, :].astype(f32) + Rz[0, 3, rows, :].astype(f32) + Rz[1, 3, rows, :].astype(f32)).astype(bf16)

    def unpack():
        def piece(src, _):
            v = HR[src].astype(f32)
            upper = jnp.concatenate([v[:8, :768], v[8:, :768]], 1)
            lower = jnp.concatenate([v[4 * q:4 * q + 4, 768:] for q in range(4)], 1)
            hid_out[:, pl.ds(pl.multiple_of(src * 1536, 1536), 1536)] = jnp.concatenate([upper, lower], 0).astype(bf16)
            return 0

        lax.fori_loop(0, 16, piece, 0)

    def finish_hidden():
        recv_hidden(4, 3, -3, 2, -2, 1, -1, 0)
        keep.wait()
        unpack()

    steps = dict(hid=send_hidden, qx1=qx1, qx2=qx2, qx_end=qx_end, qy=lambda hop: qy(hop) if hop > 1 else qy1(), qy_end=qy_end,
                 gy=lambda hop, p: gy(hop, p) if hop > 1 else gy1(p), gy_end=gy_end, gx1=gx1, gx2=gx2, gx_end=gx_end,
                 dks=dk_send, dz1=dz1, dz=dz, dz_end=dz_end, fin=finish_hidden)
    early, mail.sent = mail.sent, []
    steps["drain"] = lambda: mail.drain(like, kdev, early)
    parts2 = split(backward_order, [(u, r) for r in range(8) for u in ("T", "P")])

    def backward_round(r, _):
        for work, offset in ((terms, 0), (partial, 1)):
            for i in range(8):
                if parts2[2 * i + offset]:
                    pl.when(r == i)(functools.partial(run, steps, parts2[2 * i + offset]))
            work(r)
        return 0

    lax.fori_loop(0, 8, backward_round, 0)
    run(steps, parts2[16])
    mail.drain(like, kdev, mail.sent)


def fused(slots, count, w, tokens, cot):
    vm = pl.BlockSpec(memory_space=pltpu.VMEM)
    sm = pl.BlockSpec(memory_space=pltpu.SMEM)
    hbm = pl.BlockSpec(memory_space=pltpu.HBM)
    V = pltpu.VMEM
    n = 256
    brows = 512 - acut
    return pl.pallas_call(
        kernel_body, name="block_sparse_ffn",
        out_shape=(
            jax.ShapeDtypeStruct((12, 24576), bf16),
            jax.ShapeDtypeStruct((192, 512), bf16),
            jax.ShapeDtypeStruct((512, 128), bf16),
        ),
        in_specs=[sm, sm, hbm, hbm, hbm], out_specs=(vm, vm, vm),
        scratch_shapes=[
            V((8, 4, wrows, 128), bf16), V((8, 2, 192, 512), bf16), V((192, 1536), f32),
            V((8, 4, 8, 128), jnp.int32), pltpu.SMEM((8, 4, 8, 128), jnp.int32),
            V((17, 128, 128), bf16), V((192, 1536), f32), V((12, 192, 128), bf16), V((192, 128), f32),
            V((16, 16, 1152), f32), V((16, 16, 1152), bf16), V((16, 16, 1152), bf16),
            V((8, 4, 512, 128), bf16), V((8, 2, 192, 512), bf16),
            V((2, 4, 4, acut, 128), bf16), V((2, 2, acut, 128), bf16),
            V((2, 2, 8, brows, 128), bf16), V((2, 4, brows, 128), bf16),
            V((8, 192, 512), bf16), V((2, 4, 192, 512), bf16),
            pltpu.SemaphoreType.DMA((n,)), pltpu.SemaphoreType.DMA((n,)),
            pltpu.SemaphoreType.DMA((4,)), pltpu.SemaphoreType.DMA((8,)),
        ],
        compiler_params=pltpu.CompilerParams(collective_id=0, has_side_effects=True, vmem_limit_bytes=48 * 2**20),
    )(slots, count, w, tokens, cot)


def place_body(*refs):
    n = len(refs) // 2
    copies = [pltpu.make_async_copy(refs[i], refs[n + i], refs[-1].at[i]) for i in range(n)]
    for c in copies:
        c.start()
    for c in copies:
        c.wait()


def place(*arrays):
    return pl.pallas_call(
        place_body, name="place",
        out_shape=[jax.ShapeDtypeStruct(a.shape, a.dtype) for a in arrays],
        in_specs=[pl.BlockSpec(memory_space=pltpu.VMEM)] * len(arrays),
        out_specs=[pl.BlockSpec(memory_space=pltpu.HBM)] * len(arrays),
        scratch_shapes=[pltpu.SemaphoreType.DMA((len(arrays),))],
        compiler_params=pltpu.CompilerParams(vmem_limit_bytes=8 * 2**20),
    )(*arrays)


def body(tokens, weight_blocks, block_slots, block_counts, cotangent):
    hidden, dx, dw = fused(
        pltpu.with_memory_space_constraint(block_slots.reshape(4), pltpu.HBM), block_counts.reshape(1),
        *(pltpu.with_memory_space_constraint(a, pltpu.HBM) for a in (weight_blocks.reshape(512, 128), tokens, cotangent))
    )
    hidden, dx, dw = place(hidden, dx, dw)
    return hidden, dx, dw.reshape(1, 1, 4, 128, 128)


def solution(mesh):
    in_specs = (
        P("row", "col"),
        P("row", "col", None, None, None),
        P("row", "col", None),
        P("row", "col"),
        P("row", "col"),
    )
    out_specs = (P(("row", "col"), None), P("row", "col"), P("row", "col", None, None, None))
    return jax.shard_map(body, mesh=mesh, in_specs=in_specs, out_specs=out_specs, check_vma=False)
```

```python
import functools
import math

import jax
import jax.numpy as jnp
from jax import lax
from jax.experimental import pallas as pl
from jax.experimental.pallas import tpu as pltpu
from jax.sharding import PartitionSpec as P

MESH = pl.DeviceIdType.MESH
ny, nx, nz, nk = 8, 4, 8, 2
both = (1, -1)
f32, bf16 = jnp.float32, jnp.bfloat16

gelu_scale = 0.7978845608028654
cubic_term = 0.044715

wrows = 528
wcut = 208
acut = 176


gather_order = [
    ("by", 0, 1, 1), ("tz", 0, 1), ("by", 0, -1, 1), ("by", 0, -1, -1), ("ax", 0, 1), ("by", 0, 1, -1), ("tz", 0, 0), ("ax", 0, -1), ("ays", 0),
    ("tz", 0, 2), ("bxs", 0, -1), ("tz", 0, 3), ("bxs", 0, 1), ("by", 1, 1, 1), ("bxs", -1, 1), ("by", 1, -1, 1), ("tz", 1, 1), ("ax", 1, 1),
    ("by", 1, 1, -1), ("ax", 1, -1), ("by", 1, -1, -1), ("bxs", 1, -1), ("ays", 1), ("bxs", 1, 1), ("tz", 1, 0), ("ays", 2), ("tz", 1, 2),
    ("bxs", -1, -1), ("tz", 1, 3), ("bx1", 0, 1), ("by", 2, 1, 1), ("bx1", 0, -1), ("by", 2, -1, 1), ("bxs", -2, 1), ("by", 2, 1, -1), ("bxs", -2, -1),
    ("by", 2, -1, -1), ("tz", 2, 1), ("ax2",), ("ays", 3), ("tz", 2, 0), ("bx1", 1, -1), ("ay", 1, 0, -1), ("bxs", 2, -1), ("tz", 2, 2),
    ("ay", 1, 0, 1), ("bxs", 2, 1), ("bx1", 1, 1), ("tz", 2, 3), ("by", 3, 1, 1), ("bx1", -1, 1), ("bxs", -3, 1), ("tk", -2), ("by", 3, 1, -1),
    ("bx1", -1, -1), ("tk", 2), ("by", 3, -1, 1), ("by", 3, -1, -1), ("bx2", 0), ("tz", 3, 1), ("ay", 1, 1, 1), ("ay", 1, 1, -1), ("tz", 3, 0),
    ("bxs", -3, -1), ("tz", 3, 2), ("bx1", 2, -1), ("tz", 3, 3), ("bxs", 3, 1), ("ay", 2, 0, -1), ("tk", 3), ("tk", 1), ("ay", 2, 0, 1), ("bx2", 1),
    ("tk", -3), ("bxs", 3, -1), ("bx1", -2, -1), ("by", 4, 1, 1), ("bx1", 2, 1), ("tz", 4, 1), ("tk", 0), ("codes", 0), ("codes", 1), ("bxs", 4, 1),
    ("bx1", -2, 1), ("tk", -1), ("by", 4, -1, -1), ("bx2", -1), ("tz", 4, 0), ("tk", 4), ("bxs", 4, -1), ("bx1", -3, 1), ("codes", 2), ("bx1", -3, -1),
    ("ay", 2, 1, 1), ("ay", 2, 1, -1), ("tk_end",), ("apply", 0), ("apply", 1), ("bx1", 3, 1), ("bx2", 2), ("ay", 3, 0, -1), ("ay", 3, 0, 1),
    ("bx1", 3, -1), ("codes", 3), ("apply", 2), ("bx1", 4, 1), ("apply", 3), ("ay", 3, 1, 1), ("bx1", 4, -1), ("ay", 3, 1, -1), ("bx2", -2),
    ("codes", 4), ("apply", 4), ("bx2", -3), ("codes", 6), ("bx2", 3), ("codes", 5), ("apply", 5), ("apply", 6), ("bx2", 4), ("ay4",), ("codes", 7),
    ("apply", 7),
]
backward_order = [
    ("hid", 4), ("T", 0), ("qx1", 4), ("gy", 1, 1), ("P", 0), ("dks", 4), ("gy", 1, 0), ("T", 1), ("qx1", 3), ("P", 1), ("dz1",), ("T", 2),
    ("qx1", -3), ("P", 2), ("hid", -3), ("qx2", 4), ("gy", 2, 1), ("T", 3), ("dks", 3), ("dks", -3), ("hid", 1), ("qx1", 2), ("qx2", 3), ("P", 3),
    ("gy", 2, 0), ("dz", 2, 1), ("T", 4), ("qx2", -3), ("dz", 2, -1), ("qx_end", 4), ("qy", 1), ("qx1", -2), ("gy", 3, 1), ("P", 4), ("qx2", 2),
    ("hid", 2), ("T", 5), ("gy", 3, 0), ("qx1", 1), ("dks", 2), ("P", 5), ("T", 6), ("qx_end", 3), ("hid", -2), ("qx_end", -3), ("qy", 2), ("dks", 1),
    ("qx1", -1), ("dks", -2), ("dz", 3, 1), ("qx2", -2), ("gy", 4, 1), ("hid", 3), ("P", 6), ("T", 7), ("qx1", 0), ("dz", 3, -1), ("gy", 4, 0),
    ("qx2", 1), ("hid", -1), ("qx_end", 2), ("qx2", -1), ("qx_end", -2), ("dks", -1), ("qy", 3), ("P", 7), ("dz", 4, 1), ("gy_end", 1), ("gy_end", 0),
    ("gx1",), ("drain",), ("qx2", 0), ("dz", 4, -1), ("qx_end", 1), ("qx_end", -1), ("qy", 4), ("gx2",), ("hid", 0), ("dks", 0), ("qx_end", 0),
    ("fin",), ("qy_end",), ("gx_end",), ("dz_end",),
]


def gelu_pair(v):
    inner = gelu_scale * (v + cubic_term * v * v * v)
    th = jnp.tanh(inner)
    act = 0.5 * v * (1.0 + th)
    der = 0.5 * (1.0 + th) + 0.5 * v * (1.0 - th * th) * gelu_scale * (1.0 + 3.0 * cubic_term * v * v)
    return act, der


def wrap(v, n):
    return lax.rem(v + n, n)


def halves(start, rows):
    upper = (rows // 2 + 15) // 16 * 16
    return {1: pl.ds(start, upper), -1: pl.ds(start + upper, rows - upper)}


def split(order, marks):
    cuts = [-1] + [order.index(m) for m in marks] + [len(order)]
    return [order[a + 1:b] for a, b in zip(cuts, cuts[1:])]


def run(steps, part):
    for name, *args in part:
        steps[name](*args)


class Mail:
    def __init__(self, send_sem, recv_sem):
        self.send_sem, self.recv_sem = send_sem, recv_sem
        self.ids = {}
        self.sent = []

    def copy(self, name, src, dst, to):
        i = self.ids.setdefault(name, len(self.ids))
        return pltpu.make_async_remote_copy(
            src_ref=src, dst_ref=dst, send_sem=self.send_sem.at[i], recv_sem=self.recv_sem.at[i],
            device_id=to, device_id_type=MESH,
        )

    def send(self, name, src, dst, to):
        self.copy(name, src, dst, to).start()
        self.sent.append((name, tuple(src.shape)))

    def recv(self, name, dst, to):
        self.copy(name, dst, dst, to).wait_recv()

    def drain(self, like, to, sent):
        for name, shape in sent:
            self.copy(name, like(shape), like(shape), to).wait_send()


def kernel_body(
    slot_in, count_in, w_ref, tok_ref, cot_ref,
    hid_out, dx_out, dw_out,
    W, T, cot, code_v, code, blocks, pre, gp, act_s, Hs, H, HR, G, D,
    Ray, Rax, Rbx, Rby, Rk, Rz,
    slot_ref, count_ref, send_sem, recv_sem, own_sem, code_sem,
):
    r_me, c_me = lax.axis_index("row"), lax.axis_index("col")
    y, x, z, k = r_me // nx, lax.rem(r_me, nx), c_me // nk, lax.rem(c_me, nk)

    def device(yi, xi, zi, ki):
        return (yi * nx + xi, zi * nk + ki)

    own = [
        pltpu.make_async_copy(w_ref, W.at[y, x, pl.ds(0, 512)], own_sem.at[0]),
        pltpu.make_async_copy(tok_ref, T.at[z, k], own_sem.at[1]),
        pltpu.make_async_copy(cot_ref, cot, own_sem.at[2]),
        pltpu.make_async_copy(slot_in, slot_ref, own_sem.at[4]),
        pltpu.make_async_copy(count_in, count_ref, own_sem.at[5]),
    ]
    for c in own:
        c.start()

    yy = lambda d: wrap(y + d, ny)
    xx = lambda d: wrap(x + d, nx)
    zz = lambda d: wrap(z + d, nz)
    ydev = {s: device(yy(s), x, z, k) for s in both}
    xdev = {s: device(y, xx(s), z, k) for s in both}
    zdev = {s: device(y, x, zz(s), k) for s in both}
    kdev = device(y, x, z, 1 - k)

    bar = pltpu.get_barrier_semaphore()
    peers = [ydev[1], ydev[-1], xdev[1], xdev[-1], zdev[1], zdev[-1], kdev]
    for p in peers:
        pl.semaphore_signal(bar, inc=1, device_id=p, device_id_type=MESH)

    own[3].wait()
    own[4].wait()
    line = lax.broadcasted_iota(jnp.int32, (16, 128), 0)
    numbers = jnp.zeros((16, 128), f32)
    for s in range(4):
        number = jnp.where(s < count_ref[0], slot_ref[s], slot_ref[s] + 24)
        numbers = jnp.where(line == s, number.astype(f32), numbers)
    W[y, x, 512:528, :] = numbers.astype(bf16)
    pre[...] = jnp.zeros_like(pre)
    blocks[16] = jnp.zeros((128, 128), bf16)
    own[0].wait()
    own[1].wait()
    pl.semaphore_wait(bar, len(peers))

    mail = Mail(send_sem, recv_sem)

    def like(shape):
        if shape[-1] == 512:
            return T.at[0, 0, pl.ds(0, shape[0])]
        if shape[-1] == 1152:
            return H.at[0]
        if len(shape) == 3:
            return W.at[0, pl.ds(0, shape[0]), pl.ds(0, shape[1])]
        return W.at[0, 0, pl.ds(0, shape[0])]

    A = pl.ds(0, wcut)
    B = pl.ds(wcut, wrows - wcut)
    ha = halves(0, wcut)
    hb = halves(wcut, wrows - wcut)
    side = 1 - 2 * lax.rem(x, 2)
    pair = {0: pl.ds(2 * (x // 2), 2), 1: pl.ds(2 * (1 - x // 2), 2)}
    role_x = {0: x, 1: xx(side), 2: xx(-side), 3: xx(2)}
    chunk = {s: [pl.ds(48 * i, 48) for i in ((0, 1, 2, 3) if s == 1 else (2, 3, 0, 1))] for s in both}

    def by(hop, s, c):
        piece = W.at[yy(-s * hop), x, hb[c]]
        if hop > 0:
            mail.recv(f"by{hop}{s}c{c}", piece, ydev[s])
        if hop < 3 or (hop == 3 and c == s):
            mail.send(f"by{hop + 1}{s}c{c}", piece, piece, ydev[s])

    def bxs(d, c):
        piece = W.at[yy(d), x, hb[c]]
        for t in both:
            mail.send(f"bx1{t}y{d}c{c}", piece, piece, xdev[t])

    def bx1(d, c):
        for t in both:
            piece = W.at[yy(d), xx(-t), hb[c]]
            mail.recv(f"bx1{t}y{d}c{c}", piece, xdev[t])
            if t == c:
                mail.send(f"bx2{t}y{d}", piece, piece, xdev[t])

    def bx2(d):
        for t in both:
            mail.recv(f"bx2{t}y{d}", W.at[yy(d), xx(2), hb[t]], xdev[t])

    def ax(hop, t):
        if hop == 0:
            mail.send(f"ax1{t}", W.at[y, x, A], W.at[y, x, A], xdev[t])
            return
        mail.recv(f"ax1{t}", W.at[y, xx(-t), A], xdev[t])
        half = W.at[y, xx(-t), ha[t]]
        mail.send(f"ax2{t}", half, half, xdev[t])

    def ax2():
        for t in both:
            mail.recv(f"ax2{t}", W.at[y, xx(2), ha[t]], xdev[t])

    def ays(role):
        piece = W.at[y, role_x[role], A]
        for s in both:
            mail.send(f"ay1{s}r{role}", piece, piece, ydev[s])

    def ay(hop, p, s):
        piece = W.at[yy(-s * hop), pair[p], A]
        if hop == 1:
            for role in (2 * p, 2 * p + 1):
                mail.recv(f"ay1{s}r{role}", W.at[yy(-s), role_x[role], A], ydev[s])
        else:
            mail.recv(f"ay{hop}{s}p{p}", piece, ydev[s])
        if hop < 3:
            mail.send(f"ay{hop + 1}{s}p{p}", piece, piece, ydev[s])
        else:
            half = W.at[yy(-s * hop), pair[p], ha[s]]
            mail.send(f"ay4{s}p{p}", half, half, ydev[s])

    def ay4():
        for p in range(2):
            for s in both:
                mail.recv(f"ay4{s}p{p}", W.at[yy(4), pair[p], ha[s]], ydev[s])

    def tz(hop, i):
        for s in both:
            piece = T.at[zz(-s * hop), k, chunk[s][i]]
            if 0 < hop < 4 or (hop == 4 and i < 2):
                mail.recv(f"tz{hop}{s}c{i}", piece, zdev[s])
            if hop < 3 or (hop == 3 and i < 2):
                mail.send(f"tz{hop + 1}{s}c{i}", piece, piece, zdev[s])

    def tk(d):
        mail.send(f"tk{d}", T.at[zz(d), k], T.at[zz(d), k], kdev)

    def tk_end():
        for d in (0, 1, -1, 2, -2, 3, -3, 4):
            mail.recv(f"tk{d}", T.at[zz(d), 1 - k], kdev)

    def near_first(r):
        m = (r + 1) // 2
        return m * (2 * lax.rem(r, 2) - 1)

    def codes(r):
        g = wrap(y + near_first(r), ny)
        for i in range(4):
            code_v[g, i] = W[g, i, 512:528, :][:8].astype(f32).astype(jnp.int32)
        pltpu.make_async_copy(code_v.at[g], code.at[g], code_sem.at[g]).start()

    def apply(r):
        g = wrap(y + near_first(r), ny)
        for i in range(4):
            for s in range(4):
                blocks[4 * i + s] = W[g, i, s * 128:(s + 1) * 128, :]
        pltpu.make_async_copy(code_v.at[g], code.at[g], code_sem.at[g]).wait()
        index = {}
        for i in range(4):
            n = [code[g, i, s, 0] for s in range(4)]
            for p in range(24):
                at = 16
                for s in (3, 2, 1, 0):
                    at = jnp.where(n[s] == p, 4 * i + s, at)
                index[i, p] = at
        for j in range(0, 12, 2):
            total = pre[:, j * 128:(j + 2) * 128]
            for h in range(2):
                rows = [
                    jnp.concatenate([blocks[index[i, 12 * u + j]], blocks[index[i, 12 * u + j + 1]]], 1)
                    for i in (2 * h, 2 * h + 1) for u in range(2)
                ]
                total = total + jnp.dot(T[g, h], jnp.concatenate(rows, 0), preferred_element_type=f32)
            pre[:, j * 128:(j + 2) * 128] = total

    steps = dict(by=by, bxs=bxs, bx1=bx1, bx2=bx2, ax=ax, ax2=ax2, ays=ays, ay=ay, ay4=ay4, tz=tz, tk=tk, tk_end=tk_end, codes=codes)
    parts = split(gather_order, [("apply", r) for r in range(8)])
    run(steps, parts[0])

    def gather_round(r, _):
        for i in range(1, 8):
            if parts[i]:
                pl.when(r == i)(functools.partial(run, steps, parts[i]))
        apply(r)
        return 0

    lax.fori_loop(0, 8, gather_round, 0)
    run(steps, parts[8])
    own[2].wait()

    def activation(i, _):
        for q in range(4):
            j = 3 * q + i
            cols = pl.ds(pl.multiple_of(j * 128, 128), 128)
            act, der = gelu_pair(pre[:, cols])
            gp[j] = (cot[:, cols] * der).astype(bf16)
            act_s[...] = act
            upper = pl.ds(pl.multiple_of((3 * (q % 2) + i) * 128, 128), 128)
            lower = pl.ds(pl.multiple_of(768 + i * 128, 128), 128)
            for c in range(16):
                Hs[c, 8 * (q // 2):8 * (q // 2) + 8, upper] = act_s[12 * c:12 * c + 8]
                Hs[c, 4 * q:4 * q + 4, lower] = act_s[12 * c + 8:12 * c + 12]
        return 0

    lax.fori_loop(0, 3, activation, 0)
    H[...] = Hs[...].astype(bf16)
    keep = pltpu.make_async_copy(H.at[c_me], HR.at[c_me], own_sem.at[3])
    keep.start()

    brows = 512 - acut
    A = pl.ds(0, acut)
    B = pl.ds(acut, brows)
    ha2 = halves(0, acut)
    hb2 = halves(acut, brows)
    hr = halves(0, brows)
    ht = {1: pl.ds(0, 96), -1: pl.ds(96, 96)}

    def far_first(r):
        m = (r + 1) // 2
        return (4 - m) * (2 * lax.rem(r, 2) - 1)

    def grad_cat(g, i):
        return jnp.concatenate([gp[jnp.clip(lax.rem(code[g, i, s, 0], 12), 0, 11)] for s in range(4)], 1)

    def terms(r):
        yi = wrap(y + far_first(r), ny)
        for i in range(4):
            tok = T[yi, i // 2, :, (i % 2) * 256:(i % 2 + 1) * 256]
            full = lax.dot_general(tok, grad_cat(yi, i), (((0,), (0,)), ((), ())), preferred_element_type=f32)
            for s in range(4):
                part = full[:, s * 128:(s + 1) * 128]
                G[yi, i, s * 128:(s + 1) * 128, :] = jnp.where(code[yi, i, s, 0] < 12, part[:128], part[128:]).astype(bf16)

    def partial(r):
        zi = wrap(z + far_first(r), nz)
        for i in range(4):
            top, bottom = [], []
            for s in range(4):
                w = W[zi, i, s * 128:(s + 1) * 128, :]
                n = code[zi, i, s, 0]
                top.append(jnp.where(n < 12, w, jnp.zeros_like(w)))
                bottom.append(jnp.where((n >= 12) & (n < 24), w, jnp.zeros_like(w)))
            wide = jnp.concatenate([jnp.concatenate(top, 1), jnp.concatenate(bottom, 1)], 0)
            out = lax.dot_general(grad_cat(zi, i), wide, (((1,), (1,)), ((), ())), preferred_element_type=f32)
            D[zi, i // 2, :, (i % 2) * 256:(i % 2 + 1) * 256] = out.astype(bf16)

    def send_hidden(*ds):
        for dz in ds:
            for dk in range(2):
                if dz or dk:
                    zi, ki = zz(dz), lax.rem(k + dk, 2)
                    mail.send(f"h{dz % 8}{dk}", H.at[zi * 2 + ki], HR.at[c_me], device(y, x, zi, ki))

    def recv_hidden(*ds):
        for dz in ds:
            for dk in range(2):
                if dz or dk:
                    mail.recv(f"h{dz % 8}{dk}", HR.at[zz(-dz) * 2 + lax.rem(k + dk, 2)], kdev)

    xpair = [pl.ds(0, 2), pl.ds(2, 2)]

    def gy1(p):
        for s in both:
            mail.send(f"gy1{s}p{p}", G.at[yy(4), xpair[p], ha2[s]], Ray.at[(1 - s) // 2, 0, xpair[p], ha2[s]], ydev[s])

    def gy(hop, p):
        for s in both:
            i, yi, xp = (1 - s) // 2, yy(s * (5 - hop)), xpair[p]
            rows = ha2[s] if hop == 2 else A
            mail.recv(f"gy{hop - 1}{s}p{p}", Ray.at[i, hop - 2, xp, rows], ydev[s])
            G[yi, xp, rows, :] = G[yi, xp, rows, :] + Ray[i, hop - 2, xp, rows, :]
            mail.send(f"gy{hop}{s}p{p}", G.at[yi, xp, A], Ray.at[i, hop - 1, xp, A], ydev[s])

    def gy_end(p):
        for s in both:
            mail.recv(f"gy4{s}p{p}", Ray.at[(1 - s) // 2, 3, xpair[p], A], ydev[s])
        xp = xpair[p]
        G[y, xp, A, :] = (G[y, xp, A, :].astype(f32) + Ray[0, 3, xp, A, :].astype(f32) + Ray[1, 3, xp, A, :].astype(f32)).astype(bf16)

    def gx1():
        for t in both:
            mail.send(f"gx1{t}", G.at[y, xx(2), ha2[t]], Rax.at[(1 - t) // 2, 0, ha2[t]], xdev[t])

    def gx2():
        for t in both:
            i = (1 - t) // 2
            mail.recv(f"gx1{t}", Rax.at[i, 0, ha2[t]], xdev[t])
            G[y, xx(t), ha2[t], :] = G[y, xx(t), ha2[t], :] + Rax[i, 0, ha2[t], :]
            mail.send(f"gx2{t}", G.at[y, xx(t), A], Rax.at[i, 1], xdev[t])

    def finish(rows, r0, r1):
        total = G[y, x, rows, :].astype(f32) + r0.astype(f32) + r1.astype(f32)
        row = lax.broadcasted_iota(jnp.int32, total.shape, 0) + rows.start
        usable = row < count_ref[0] * 128
        dw_out[rows, :] = jnp.where(usable, total * (1.0 / math.sqrt(6144)), 0.0).astype(bf16)

    def gx_end():
        for t in both:
            mail.recv(f"gx2{t}", Rax.at[(1 - t) // 2, 1], xdev[t])
        finish(A, Rax[0, 1], Rax[1, 1])

    def qx1(d):
        for t in both:
            mail.send(f"qx1{t}y{d}", G.at[yy(d), xx(2), hb2[t]], Rbx.at[(1 - t) // 2, 0, yy(d), hr[t]], xdev[t])

    def qx2(d):
        for t in both:
            i = (1 - t) // 2
            mail.recv(f"qx1{t}y{d}", Rbx.at[i, 0, yy(d), hr[t]], xdev[t])
            G[yy(d), xx(t), hb2[t], :] = G[yy(d), xx(t), hb2[t], :] + Rbx[i, 0, yy(d), hr[t], :]
            mail.send(f"qx2{t}y{d}", G.at[yy(d), xx(t), B], Rbx.at[i, 1, yy(d)], xdev[t])

    def qx_end(d):
        for t in both:
            mail.recv(f"qx2{t}y{d}", Rbx.at[(1 - t) // 2, 1, yy(d)], xdev[t])
        G[yy(d), x, B, :] = (G[yy(d), x, B, :].astype(f32) + Rbx[0, 1, yy(d)].astype(f32) + Rbx[1, 1, yy(d)].astype(f32)).astype(bf16)

    def qy1():
        for s in both:
            mail.send(f"qy1{s}", G.at[yy(4), x, hb2[s]], Rby.at[(1 - s) // 2, 0, hr[s]], ydev[s])

    def qy(hop):
        for s in both:
            i, yi = (1 - s) // 2, yy(s * (5 - hop))
            rows, inner = (hb2[s], hr[s]) if hop == 2 else (B, pl.ds(0, brows))
            mail.recv(f"qy{hop - 1}{s}", Rby.at[i, hop - 2, inner], ydev[s])
            G[yi, x, rows, :] = G[yi, x, rows, :] + Rby[i, hop - 2, inner, :]
            mail.send(f"qy{hop}{s}", G.at[yi, x, B], Rby.at[i, hop - 1], ydev[s])

    def qy_end():
        for s in both:
            mail.recv(f"qy4{s}", Rby.at[(1 - s) // 2, 3], ydev[s])
        finish(B, Rby[0, 3], Rby[1, 3])

    def dk_send(d):
        mail.send(f"dk{d}", D.at[zz(d), 1 - k], Rk.at[zz(d)], kdev)

    def dk_add(d):
        mail.recv(f"dk{d}", Rk.at[zz(d)], kdev)
        D[zz(d), k] = D[zz(d), k] + Rk[zz(d)]

    def dz1():
        dk_add(4)
        for s in both:
            mail.send(f"dz1{s}h{s}", D.at[zz(4), k, ht[s]], Rz.at[(1 - s) // 2, 0, ht[s]], zdev[s])

    def dz(hop, s):
        i, d = (1 - s) // 2, s * (5 - hop)
        dk_add(d)
        zi = zz(d)
        for h in ((-s, s) if hop == 2 else (s, -s)):
            rows = ht[h]
            if hop > 2 or h == s:
                mail.recv(f"dz{hop - 1}{s}h{h}", Rz.at[i, hop - 2, rows], zdev[s])
                D[zi, k, rows, :] = D[zi, k, rows, :] + Rz[i, hop - 2, rows, :]
            mail.send(f"dz{hop}{s}h{h}", D.at[zi, k, rows], Rz.at[i, hop - 1, rows], zdev[s])

    def dz_end():
        dk_add(0)
        for h in both:
            for s in both:
                mail.recv(f"dz4{s}h{h}", Rz.at[(1 - s) // 2, 3, ht[h]], zdev[s])
            rows = ht[h]
            dx_out[rows, :] = (D[z, k, rows, :].astype(f32) + Rz[0, 3, rows, :].astype(f32) + Rz[1, 3, rows, :].astype(f32)).astype(bf16)

    def unpack():
        def piece(src, _):
            v = HR[src].astype(f32)
            upper = jnp.concatenate([v[:8, :768], v[8:, :768]], 1)
            lower = jnp.concatenate([v[4 * q:4 * q + 4, 768:] for q in range(4)], 1)
            hid_out[:, pl.ds(pl.multiple_of(src * 1536, 1536), 1536)] = jnp.concatenate([upper, lower], 0).astype(bf16)
            return 0

        lax.fori_loop(0, 16, piece, 0)

    def finish_hidden():
        recv_hidden(4, 3, -3, 2, -2, 1, -1, 0)
        keep.wait()
        unpack()

    steps = dict(hid=send_hidden, qx1=qx1, qx2=qx2, qx_end=qx_end, qy=lambda hop: qy(hop) if hop > 1 else qy1(), qy_end=qy_end,
                 gy=lambda hop, p: gy(hop, p) if hop > 1 else gy1(p), gy_end=gy_end, gx1=gx1, gx2=gx2, gx_end=gx_end,
                 dks=dk_send, dz1=dz1, dz=dz, dz_end=dz_end, fin=finish_hidden)
    early, mail.sent = mail.sent, []
    steps["drain"] = lambda: mail.drain(like, kdev, early)
    parts2 = split(backward_order, [(u, r) for r in range(8) for u in ("T", "P")])

    def backward_round(r, _):
        for work, offset in ((terms, 0), (partial, 1)):
            for i in range(8):
                if parts2[2 * i + offset]:
                    pl.when(r == i)(functools.partial(run, steps, parts2[2 * i + offset]))
            work(r)
        return 0

    lax.fori_loop(0, 8, backward_round, 0)
    run(steps, parts2[16])
    mail.drain(like, kdev, mail.sent)


def fused(slots, count, w, tokens, cot):
    vm = pl.BlockSpec(memory_space=pltpu.VMEM)
    hbm = pl.BlockSpec(memory_space=pltpu.HBM)
    V = pltpu.VMEM
    n = 256
    brows = 512 - acut
    return pl.pallas_call(
        kernel_body, name="block_sparse_ffn",
        out_shape=(
            jax.ShapeDtypeStruct((12, 24576), bf16),
            jax.ShapeDtypeStruct((192, 512), bf16),
            jax.ShapeDtypeStruct((512, 128), bf16),
        ),
        in_specs=[hbm] * 5, out_specs=(vm, vm, vm),
        scratch_shapes=[
            V((8, 4, wrows, 128), bf16), V((8, 2, 192, 512), bf16), V((192, 1536), f32),
            V((8, 4, 8, 128), jnp.int32), pltpu.SMEM((8, 4, 8, 128), jnp.int32),
            V((17, 128, 128), bf16), V((192, 1536), f32), V((12, 192, 128), bf16), V((192, 128), f32),
            V((16, 16, 1152), f32), V((16, 16, 1152), bf16), V((16, 16, 1152), bf16),
            V((8, 4, 512, 128), bf16), V((8, 2, 192, 512), bf16),
            V((2, 4, 4, acut, 128), bf16), V((2, 2, acut, 128), bf16),
            V((2, 2, 8, brows, 128), bf16), V((2, 4, brows, 128), bf16),
            V((8, 192, 512), bf16), V((2, 4, 192, 512), bf16),
            pltpu.SMEM((4,), jnp.int32), pltpu.SMEM((1,), jnp.int32),
            pltpu.SemaphoreType.DMA((n,)), pltpu.SemaphoreType.DMA((n,)),
            pltpu.SemaphoreType.DMA((6,)), pltpu.SemaphoreType.DMA((8,)),
        ],
        compiler_params=pltpu.CompilerParams(collective_id=0, has_side_effects=True, vmem_limit_bytes=48 * 2**20),
    )(slots, count, w, tokens, cot)


def place_body(*refs):
    n = len(refs) // 2
    copies = [pltpu.make_async_copy(refs[i], refs[n + i], refs[-1].at[i]) for i in range(n)]
    for c in copies:
        c.start()
    for c in copies:
        c.wait()


def place(*arrays):
    return pl.pallas_call(
        place_body, name="place",
        out_shape=[jax.ShapeDtypeStruct(a.shape, a.dtype) for a in arrays],
        in_specs=[pl.BlockSpec(memory_space=pltpu.VMEM)] * len(arrays),
        out_specs=[pl.BlockSpec(memory_space=pltpu.HBM)] * len(arrays),
        scratch_shapes=[pltpu.SemaphoreType.DMA((len(arrays),))],
        compiler_params=pltpu.CompilerParams(vmem_limit_bytes=8 * 2**20),
    )(*arrays)


def body(tokens, weight_blocks, block_slots, block_counts, cotangent):
    hidden, dx, dw = fused(
        pltpu.with_memory_space_constraint(block_slots.reshape(4), pltpu.HBM), block_counts.reshape(1),
        *(pltpu.with_memory_space_constraint(a, pltpu.HBM) for a in (weight_blocks.reshape(512, 128), tokens, cotangent))
    )
    hidden, dx, dw = place(hidden, dx, dw)
    return hidden, dx, dw.reshape(1, 1, 4, 128, 128)


def solution(mesh):
    in_specs = (
        P("row", "col"),
        P("row", "col", None, None, None),
        P("row", "col", None),
        P("row", "col"),
        P("row", "col"),
    )
    out_specs = (P(("row", "col"), None), P("row", "col"), P("row", "col", None, None, None))
    return jax.shard_map(body, mesh=mesh, in_specs=in_specs, out_specs=out_specs, check_vma=False)
```

```python
import functools
import math

import jax
import jax.numpy as jnp
from jax import lax
from jax.experimental import pallas as pl
from jax.experimental.pallas import tpu as pltpu
from jax.sharding import PartitionSpec as P

MESH = pl.DeviceIdType.MESH
ny, nx, nz, nk = 8, 4, 8, 2
both = (1, -1)
f32, bf16 = jnp.float32, jnp.bfloat16

gelu_scale = 0.7978845608028654
cubic_term = 0.044715

wrows = 528
wcut = 208
acut = 160


gather_order = [
    ("by", 0, 1, 1), ("tz", 0, 1), ("by", 0, -1, 1), ("by", 0, -1, -1), ("ax", 0, 1), ("by", 0, 1, -1), ("tz", 0, 0), ("ax", 0, -1), ("ays", 0),
    ("tz", 0, 2), ("bxs", 0, -1), ("tz", 0, 3), ("bxs", 0, 1), ("by", 1, 1, 1), ("bxs", -1, 1), ("by", 1, -1, 1), ("tz", 1, 1), ("ax", 1, 1),
    ("by", 1, 1, -1), ("ax", 1, -1), ("by", 1, -1, -1), ("bxs", 1, -1), ("ays", 1), ("bxs", 1, 1), ("tz", 1, 0), ("ays", 2), ("tz", 1, 2),
    ("bxs", -1, -1), ("tz", 1, 3), ("bx1", 0, 1), ("by", 2, 1, 1), ("bx1", 0, -1), ("by", 2, -1, 1), ("bxs", -2, 1), ("by", 2, 1, -1), ("bxs", -2, -1),
    ("by", 2, -1, -1), ("tz", 2, 1), ("ax2",), ("ays", 3), ("tz", 2, 0), ("bx1", 1, -1), ("ay", 1, 0, -1), ("bxs", 2, -1), ("tz", 2, 2),
    ("ay", 1, 0, 1), ("bxs", 2, 1), ("bx1", 1, 1), ("tz", 2, 3), ("by", 3, 1, 1), ("bx1", -1, 1), ("bxs", -3, 1), ("tk", -2), ("by", 3, 1, -1),
    ("bx1", -1, -1), ("tk", 2), ("by", 3, -1, 1), ("by", 3, -1, -1), ("bx2", 0), ("tz", 3, 1), ("ay", 1, 1, 1), ("ay", 1, 1, -1), ("tz", 3, 0),
    ("bxs", -3, -1), ("tz", 3, 2), ("bx1", 2, -1), ("tz", 3, 3), ("bxs", 3, 1), ("ay", 2, 0, -1), ("tk", 3), ("tk", 1), ("ay", 2, 0, 1), ("bx2", 1),
    ("tk", -3), ("bxs", 3, -1), ("bx1", -2, -1), ("by", 4, 1, 1), ("bx1", 2, 1), ("tz", 4, 1), ("tk", 0), ("codes", 0), ("codes", 1), ("bxs", 4, 1),
    ("bx1", -2, 1), ("tk", -1), ("by", 4, -1, -1), ("bx2", -1), ("tz", 4, 0), ("tk", 4), ("bxs", 4, -1), ("bx1", -3, 1), ("codes", 2), ("bx1", -3, -1),
    ("ay", 2, 1, 1), ("ay", 2, 1, -1), ("tk_end",), ("apply", 0), ("apply", 1), ("bx1", 3, 1), ("bx2", 2), ("ay", 3, 0, -1), ("ay", 3, 0, 1),
    ("bx1", 3, -1), ("codes", 3), ("apply", 2), ("bx1", 4, 1), ("apply", 3), ("ay", 3, 1, 1), ("bx1", 4, -1), ("ay", 3, 1, -1), ("bx2", -2),
    ("codes", 4), ("apply", 4), ("bx2", -3), ("codes", 6), ("bx2", 3), ("codes", 5), ("apply", 5), ("apply", 6), ("bx2", 4), ("ay4",), ("codes", 7),
    ("apply", 7),
]
backward_order = [
    ("hid", -3), ("hid", 3), ("T", 0), ("qx1", 4), ("gy", 1, 1), ("P", 0), ("T", 1), ("qx1", 3), ("dks", 4), ("gy", 1, 0), ("P", 1), ("T", 2),
    ("qx1", -3), ("P", 2), ("dz1",), ("qx2", 4), ("gy", 2, 1), ("T", 3), ("P", 3), ("hid", 2), ("dks", -3), ("qx1", 2), ("hid", -1), ("T", 4),
    ("qx1", -2), ("qx2", -3), ("dks", 3), ("gy", 2, 0), ("qx2", 3), ("dz", 2, -1), ("gy", 3, 1), ("dz", 2, 1), ("P", 4), ("qx2", 2), ("hid", 4),
    ("qx_end", 4), ("qy", 1), ("T", 5), ("gy", 3, 0), ("dks", -2), ("P", 5), ("T", 6), ("qx1", -1), ("qx1", 1), ("qx_end", -3), ("gy", 4, 1),
    ("qx2", -2), ("hid", 0), ("dks", 2), ("qx_end", 3), ("dz", 3, -1), ("qy", 2), ("P", 6), ("T", 7), ("dz", 3, 1), ("qx1", 0), ("gy", 4, 0),
    ("dks", -1), ("qx2", -1), ("gy_end", 1), ("qx2", 1), ("hid", -2), ("qx_end", 2), ("hid", 1), ("dks", 1), ("qx_end", -2), ("qy", 3), ("P", 7),
    ("dks", 0), ("dz", 4, -1), ("gy_end", 0), ("gx1",), ("dz", 4, 1), ("drain",), ("qx2", 0), ("qx_end", -1), ("qx_end", 1), ("qy", 4), ("gx2",),
    ("fin",), ("qx_end", 0), ("dz_end",), ("gx_end",), ("qy_end",),
]


def gelu_pair(v):
    inner = gelu_scale * (v + cubic_term * v * v * v)
    th = jnp.tanh(inner)
    act = 0.5 * v * (1.0 + th)
    der = 0.5 * (1.0 + th) + 0.5 * v * (1.0 - th * th) * gelu_scale * (1.0 + 3.0 * cubic_term * v * v)
    return act, der


def wrap(v, n):
    return lax.rem(v + n, n)


def halves(start, rows):
    upper = (rows // 2 + 15) // 16 * 16
    return {1: pl.ds(start, upper), -1: pl.ds(start + upper, rows - upper)}


def split(order, marks):
    cuts = [-1] + [order.index(m) for m in marks] + [len(order)]
    return [order[a + 1:b] for a, b in zip(cuts, cuts[1:])]


def run(steps, part):
    for name, *args in part:
        steps[name](*args)


class Mail:
    def __init__(self, send_sem, recv_sem):
        self.send_sem, self.recv_sem = send_sem, recv_sem
        self.ids = {}
        self.sent = []

    def copy(self, name, src, dst, to):
        i = self.ids.setdefault(name, len(self.ids))
        return pltpu.make_async_remote_copy(
            src_ref=src, dst_ref=dst, send_sem=self.send_sem.at[i], recv_sem=self.recv_sem.at[i],
            device_id=to, device_id_type=MESH,
        )

    def send(self, name, src, dst, to):
        self.copy(name, src, dst, to).start()
        self.sent.append((name, tuple(src.shape)))

    def recv(self, name, dst, to):
        self.copy(name, dst, dst, to).wait_recv()

    def drain(self, like, to, sent):
        for name, shape in sent:
            self.copy(name, like(shape), like(shape), to).wait_send()


def kernel_body(
    slot_in, count_in, w_ref, tok_ref, cot_ref,
    hid_out, dx_out, dw_out,
    W, T, cot, code_v, code, blocks, pre, gp, act_s, Hs, H, HR, G, D,
    Ray, Rax, Rbx, Rby, Rk, Rz,
    slot_ref, count_ref, send_sem, recv_sem, own_sem, code_sem,
):
    r_me, c_me = lax.axis_index("row"), lax.axis_index("col")
    y, x, z, k = r_me // nx, lax.rem(r_me, nx), c_me // nk, lax.rem(c_me, nk)

    def device(yi, xi, zi, ki):
        return (yi * nx + xi, zi * nk + ki)

    own = [
        pltpu.make_async_copy(w_ref, W.at[y, x, pl.ds(0, 512)], own_sem.at[0]),
        pltpu.make_async_copy(tok_ref, T.at[z, k], own_sem.at[1]),
        pltpu.make_async_copy(cot_ref, cot, own_sem.at[2]),
        pltpu.make_async_copy(slot_in, slot_ref, own_sem.at[4]),
        pltpu.make_async_copy(count_in, count_ref, own_sem.at[5]),
    ]
    for c in own:
        c.start()

    yy = lambda d: wrap(y + d, ny)
    xx = lambda d: wrap(x + d, nx)
    zz = lambda d: wrap(z + d, nz)
    ydev = {s: device(yy(s), x, z, k) for s in both}
    xdev = {s: device(y, xx(s), z, k) for s in both}
    zdev = {s: device(y, x, zz(s), k) for s in both}
    kdev = device(y, x, z, 1 - k)

    bar = pltpu.get_barrier_semaphore()
    peers = [ydev[1], ydev[-1], xdev[1], xdev[-1], zdev[1], zdev[-1], kdev]
    for p in peers:
        pl.semaphore_signal(bar, inc=1, device_id=p, device_id_type=MESH)

    own[3].wait()
    own[4].wait()
    line = lax.broadcasted_iota(jnp.int32, (16, 128), 0)
    numbers = jnp.zeros((16, 128), f32)
    for s in range(4):
        number = jnp.where(s < count_ref[0], slot_ref[s], slot_ref[s] + 24)
        numbers = jnp.where(line == s, number.astype(f32), numbers)
    W[y, x, 512:528, :] = numbers.astype(bf16)
    pre[...] = jnp.zeros_like(pre)
    blocks[16] = jnp.zeros((128, 128), bf16)
    own[0].wait()
    own[1].wait()
    pl.semaphore_wait(bar, len(peers))

    mail = Mail(send_sem, recv_sem)

    def like(shape):
        if shape[-1] == 512:
            return T.at[0, 0, pl.ds(0, shape[0])]
        if shape[-1] == 1152:
            return H.at[0]
        if len(shape) == 3:
            return W.at[0, pl.ds(0, shape[0]), pl.ds(0, shape[1])]
        return W.at[0, 0, pl.ds(0, shape[0])]

    A = pl.ds(0, wcut)
    B = pl.ds(wcut, wrows - wcut)
    ha = halves(0, wcut)
    hb = halves(wcut, wrows - wcut)
    side = 1 - 2 * lax.rem(x, 2)
    pair = {0: pl.ds(2 * (x // 2), 2), 1: pl.ds(2 * (1 - x // 2), 2)}
    role_x = {0: x, 1: xx(side), 2: xx(-side), 3: xx(2)}
    chunk = {s: [pl.ds(48 * i, 48) for i in ((0, 1, 2, 3) if s == 1 else (2, 3, 0, 1))] for s in both}

    def by(hop, s, c):
        piece = W.at[yy(-s * hop), x, hb[c]]
        if hop > 0:
            mail.recv(f"by{hop}{s}c{c}", piece, ydev[s])
        if hop < 3 or (hop == 3 and c == s):
            mail.send(f"by{hop + 1}{s}c{c}", piece, piece, ydev[s])

    def bxs(d, c):
        piece = W.at[yy(d), x, hb[c]]
        for t in both:
            mail.send(f"bx1{t}y{d}c{c}", piece, piece, xdev[t])

    def bx1(d, c):
        for t in both:
            piece = W.at[yy(d), xx(-t), hb[c]]
            mail.recv(f"bx1{t}y{d}c{c}", piece, xdev[t])
            if t == c:
                mail.send(f"bx2{t}y{d}", piece, piece, xdev[t])

    def bx2(d):
        for t in both:
            mail.recv(f"bx2{t}y{d}", W.at[yy(d), xx(2), hb[t]], xdev[t])

    def ax(hop, t):
        if hop == 0:
            mail.send(f"ax1{t}", W.at[y, x, A], W.at[y, x, A], xdev[t])
            return
        mail.recv(f"ax1{t}", W.at[y, xx(-t), A], xdev[t])
        half = W.at[y, xx(-t), ha[t]]
        mail.send(f"ax2{t}", half, half, xdev[t])

    def ax2():
        for t in both:
            mail.recv(f"ax2{t}", W.at[y, xx(2), ha[t]], xdev[t])

    def ays(role):
        piece = W.at[y, role_x[role], A]
        for s in both:
            mail.send(f"ay1{s}r{role}", piece, piece, ydev[s])

    def ay(hop, p, s):
        piece = W.at[yy(-s * hop), pair[p], A]
        if hop == 1:
            for role in (2 * p, 2 * p + 1):
                mail.recv(f"ay1{s}r{role}", W.at[yy(-s), role_x[role], A], ydev[s])
        else:
            mail.recv(f"ay{hop}{s}p{p}", piece, ydev[s])
        if hop < 3:
            mail.send(f"ay{hop + 1}{s}p{p}", piece, piece, ydev[s])
        else:
            half = W.at[yy(-s * hop), pair[p], ha[s]]
            mail.send(f"ay4{s}p{p}", half, half, ydev[s])

    def ay4():
        for p in range(2):
            for s in both:
                mail.recv(f"ay4{s}p{p}", W.at[yy(4), pair[p], ha[s]], ydev[s])

    def tz(hop, i):
        for s in both:
            piece = T.at[zz(-s * hop), k, chunk[s][i]]
            if 0 < hop < 4 or (hop == 4 and i < 2):
                mail.recv(f"tz{hop}{s}c{i}", piece, zdev[s])
            if hop < 3 or (hop == 3 and i < 2):
                mail.send(f"tz{hop + 1}{s}c{i}", piece, piece, zdev[s])

    def tk(d):
        mail.send(f"tk{d}", T.at[zz(d), k], T.at[zz(d), k], kdev)

    def tk_end():
        for d in (0, 1, -1, 2, -2, 3, -3, 4):
            mail.recv(f"tk{d}", T.at[zz(d), 1 - k], kdev)

    def near_first(r):
        m = (r + 1) // 2
        return m * (2 * lax.rem(r, 2) - 1)

    def codes(r):
        g = wrap(y + near_first(r), ny)
        line8 = lax.broadcasted_iota(jnp.int32, (8, 128), 0)
        lane8 = lax.broadcasted_iota(jnp.int32, (8, 128), 1)
        for i in range(4):
            n = W[g, i, 512:528, :][:8].astype(f32).astype(jnp.int32)
            column = n - 12 * ((n >= 12).astype(jnp.int32) + (n >= 24).astype(jnp.int32) + (n >= 36).astype(jnp.int32))
            found = jnp.full((8, 128), 16, jnp.int32)
            for s in range(4):
                found = jnp.where(lane8 == jnp.broadcast_to(n[s:s + 1, :], (8, 128)), 4 * i + s, found)
            code_v[g, i] = jnp.where(line8 == 4, found, jnp.where(lane8 == 1, column, n))
        pltpu.make_async_copy(code_v.at[g], code.at[g], code_sem.at[g]).start()

    def apply(r):
        g = wrap(y + near_first(r), ny)
        for i in range(4):
            for s in range(4):
                blocks[4 * i + s] = W[g, i, s * 128:(s + 1) * 128, :]
        pltpu.make_async_copy(code_v.at[g], code.at[g], code_sem.at[g]).wait()
        index = {(i, p): jnp.clip(code[g, i, 4, p], 0, 16) for i in range(4) for p in range(24)}
        for j in range(0, 12, 2):
            total = pre[:, j * 128:(j + 2) * 128]
            for h in range(2):
                rows = [
                    jnp.concatenate([blocks[index[i, 12 * u + j]], blocks[index[i, 12 * u + j + 1]]], 1)
                    for i in (2 * h, 2 * h + 1) for u in range(2)
                ]
                total = total + jnp.dot(T[g, h], jnp.concatenate(rows, 0), preferred_element_type=f32)
            pre[:, j * 128:(j + 2) * 128] = total

    steps = dict(by=by, bxs=bxs, bx1=bx1, bx2=bx2, ax=ax, ax2=ax2, ays=ays, ay=ay, ay4=ay4, tz=tz, tk=tk, tk_end=tk_end, codes=codes)
    parts = split(gather_order, [("apply", r) for r in range(8)])
    run(steps, parts[0])

    def gather_round(r, _):
        for i in range(1, 8):
            if parts[i]:
                pl.when(r == i)(functools.partial(run, steps, parts[i]))
        apply(r)
        return 0

    lax.fori_loop(0, 8, gather_round, 0)
    run(steps, parts[8])
    own[2].wait()

    def activation(i, _):
        for q in range(4):
            j = 3 * q + i
            cols = pl.ds(pl.multiple_of(j * 128, 128), 128)
            act, der = gelu_pair(pre[:, cols])
            gp[j] = (cot[:, cols] * der).astype(bf16)
            act_s[...] = act
            upper = pl.ds(pl.multiple_of((3 * (q % 2) + i) * 128, 128), 128)
            lower = pl.ds(pl.multiple_of(768 + i * 128, 128), 128)
            for c in range(16):
                Hs[c, 8 * (q // 2):8 * (q // 2) + 8, upper] = act_s[12 * c:12 * c + 8]
                Hs[c, 4 * q:4 * q + 4, lower] = act_s[12 * c + 8:12 * c + 12]
        return 0

    lax.fori_loop(0, 3, activation, 0)
    H[...] = Hs[...].astype(bf16)
    keep = pltpu.make_async_copy(H.at[c_me], HR.at[c_me], own_sem.at[3])
    keep.start()

    brows = 512 - acut
    A = pl.ds(0, acut)
    B = pl.ds(acut, brows)
    ha2 = halves(0, acut)
    hb2 = halves(acut, brows)
    hr = halves(0, brows)
    ht = {1: pl.ds(0, 96), -1: pl.ds(96, 96)}

    def far_first(r):
        m = (r + 1) // 2
        return (4 - m) * (2 * lax.rem(r, 2) - 1)

    def grad_cat(g, i):
        return jnp.concatenate([gp[jnp.clip(code[g, i, s, 1], 0, 11)] for s in range(4)], 1)

    def terms(r):
        yi = wrap(y + far_first(r), ny)
        for i in range(4):
            tok = T[yi, i // 2, :, (i % 2) * 256:(i % 2 + 1) * 256]
            full = lax.dot_general(tok, grad_cat(yi, i), (((0,), (0,)), ((), ())), preferred_element_type=f32)
            for s in range(4):
                part = full[:, s * 128:(s + 1) * 128]
                G[yi, i, s * 128:(s + 1) * 128, :] = jnp.where(code[yi, i, s, 0] < 12, part[:128], part[128:]).astype(bf16)

    def partial(r):
        zi = wrap(z + far_first(r), nz)
        for i in range(4):
            top, bottom = [], []
            for s in range(4):
                w = W[zi, i, s * 128:(s + 1) * 128, :]
                n = code[zi, i, s, 0]
                top.append(jnp.where(n < 12, w, jnp.zeros_like(w)))
                bottom.append(jnp.where((n >= 12) & (n < 24), w, jnp.zeros_like(w)))
            wide = jnp.concatenate([jnp.concatenate(top, 1), jnp.concatenate(bottom, 1)], 0)
            out = lax.dot_general(grad_cat(zi, i), wide, (((1,), (1,)), ((), ())), preferred_element_type=f32)
            D[zi, i // 2, :, (i % 2) * 256:(i % 2 + 1) * 256] = out.astype(bf16)

    def send_hidden(*ds):
        for dz in ds:
            for dk in range(2):
                if dz or dk:
                    zi, ki = zz(dz), lax.rem(k + dk, 2)
                    mail.send(f"h{dz % 8}{dk}", H.at[zi * 2 + ki], HR.at[c_me], device(y, x, zi, ki))

    def recv_hidden(*ds):
        for dz in ds:
            for dk in range(2):
                if dz or dk:
                    mail.recv(f"h{dz % 8}{dk}", HR.at[zz(-dz) * 2 + lax.rem(k + dk, 2)], kdev)

    xpair = [pl.ds(0, 2), pl.ds(2, 2)]

    def gy1(p):
        for s in both:
            mail.send(f"gy1{s}p{p}", G.at[yy(4), xpair[p], ha2[s]], Ray.at[(1 - s) // 2, 0, xpair[p], ha2[s]], ydev[s])

    def gy(hop, p):
        for s in both:
            i, yi, xp = (1 - s) // 2, yy(s * (5 - hop)), xpair[p]
            rows = ha2[s] if hop == 2 else A
            mail.recv(f"gy{hop - 1}{s}p{p}", Ray.at[i, hop - 2, xp, rows], ydev[s])
            G[yi, xp, rows, :] = G[yi, xp, rows, :] + Ray[i, hop - 2, xp, rows, :]
            mail.send(f"gy{hop}{s}p{p}", G.at[yi, xp, A], Ray.at[i, hop - 1, xp, A], ydev[s])

    def gy_end(p):
        for s in both:
            mail.recv(f"gy4{s}p{p}", Ray.at[(1 - s) // 2, 3, xpair[p], A], ydev[s])
        xp = xpair[p]
        G[y, xp, A, :] = (G[y, xp, A, :].astype(f32) + Ray[0, 3, xp, A, :].astype(f32) + Ray[1, 3, xp, A, :].astype(f32)).astype(bf16)

    def gx1():
        for t in both:
            mail.send(f"gx1{t}", G.at[y, xx(2), ha2[t]], Rax.at[(1 - t) // 2, 0, ha2[t]], xdev[t])

    def gx2():
        for t in both:
            i = (1 - t) // 2
            mail.recv(f"gx1{t}", Rax.at[i, 0, ha2[t]], xdev[t])
            G[y, xx(t), ha2[t], :] = G[y, xx(t), ha2[t], :] + Rax[i, 0, ha2[t], :]
            mail.send(f"gx2{t}", G.at[y, xx(t), A], Rax.at[i, 1], xdev[t])

    def finish(rows, r0, r1):
        total = G[y, x, rows, :].astype(f32) + r0.astype(f32) + r1.astype(f32)
        row = lax.broadcasted_iota(jnp.int32, total.shape, 0) + rows.start
        usable = row < count_ref[0] * 128
        dw_out[rows, :] = jnp.where(usable, total * (1.0 / math.sqrt(6144)), 0.0).astype(bf16)

    def gx_end():
        for t in both:
            mail.recv(f"gx2{t}", Rax.at[(1 - t) // 2, 1], xdev[t])
        finish(A, Rax[0, 1], Rax[1, 1])

    def qx1(d):
        for t in both:
            mail.send(f"qx1{t}y{d}", G.at[yy(d), xx(2), hb2[t]], Rbx.at[(1 - t) // 2, 0, yy(d), hr[t]], xdev[t])

    def qx2(d):
        for t in both:
            i = (1 - t) // 2
            mail.recv(f"qx1{t}y{d}", Rbx.at[i, 0, yy(d), hr[t]], xdev[t])
            G[yy(d), xx(t), hb2[t], :] = G[yy(d), xx(t), hb2[t], :] + Rbx[i, 0, yy(d), hr[t], :]
            mail.send(f"qx2{t}y{d}", G.at[yy(d), xx(t), B], Rbx.at[i, 1, yy(d)], xdev[t])

    def qx_end(d):
        for t in both:
            mail.recv(f"qx2{t}y{d}", Rbx.at[(1 - t) // 2, 1, yy(d)], xdev[t])
        G[yy(d), x, B, :] = (G[yy(d), x, B, :].astype(f32) + Rbx[0, 1, yy(d)].astype(f32) + Rbx[1, 1, yy(d)].astype(f32)).astype(bf16)

    def qy1():
        for s in both:
            mail.send(f"qy1{s}", G.at[yy(4), x, hb2[s]], Rby.at[(1 - s) // 2, 0, hr[s]], ydev[s])

    def qy(hop):
        for s in both:
            i, yi = (1 - s) // 2, yy(s * (5 - hop))
            rows, inner = (hb2[s], hr[s]) if hop == 2 else (B, pl.ds(0, brows))
            mail.recv(f"qy{hop - 1}{s}", Rby.at[i, hop - 2, inner], ydev[s])
            G[yi, x, rows, :] = G[yi, x, rows, :] + Rby[i, hop - 2, inner, :]
            mail.send(f"qy{hop}{s}", G.at[yi, x, B], Rby.at[i, hop - 1], ydev[s])

    def qy_end():
        for s in both:
            mail.recv(f"qy4{s}", Rby.at[(1 - s) // 2, 3], ydev[s])
        finish(B, Rby[0, 3], Rby[1, 3])

    def dk_send(d):
        mail.send(f"dk{d}", D.at[zz(d), 1 - k], Rk.at[zz(d)], kdev)

    def dk_add(d):
        mail.recv(f"dk{d}", Rk.at[zz(d)], kdev)
        D[zz(d), k] = D[zz(d), k] + Rk[zz(d)]

    def dz1():
        dk_add(4)
        for s in both:
            mail.send(f"dz1{s}h{s}", D.at[zz(4), k, ht[s]], Rz.at[(1 - s) // 2, 0, ht[s]], zdev[s])

    def dz(hop, s):
        i, d = (1 - s) // 2, s * (5 - hop)
        dk_add(d)
        zi = zz(d)
        for h in ((-s, s) if hop == 2 else (s, -s)):
            rows = ht[h]
            if hop > 2 or h == s:
                mail.recv(f"dz{hop - 1}{s}h{h}", Rz.at[i, hop - 2, rows], zdev[s])
                D[zi, k, rows, :] = D[zi, k, rows, :] + Rz[i, hop - 2, rows, :]
            mail.send(f"dz{hop}{s}h{h}", D.at[zi, k, rows], Rz.at[i, hop - 1, rows], zdev[s])

    def dz_end():
        dk_add(0)
        for h in both:
            for s in both:
                mail.recv(f"dz4{s}h{h}", Rz.at[(1 - s) // 2, 3, ht[h]], zdev[s])
            rows = ht[h]
            dx_out[rows, :] = (D[z, k, rows, :].astype(f32) + Rz[0, 3, rows, :].astype(f32) + Rz[1, 3, rows, :].astype(f32)).astype(bf16)

    def unpack():
        def piece(src, _):
            v = HR[src].astype(f32)
            upper = jnp.concatenate([v[:8, :768], v[8:, :768]], 1)
            lower = jnp.concatenate([v[4 * q:4 * q + 4, 768:] for q in range(4)], 1)
            hid_out[:, pl.ds(pl.multiple_of(src * 1536, 1536), 1536)] = jnp.concatenate([upper, lower], 0).astype(bf16)
            return 0

        lax.fori_loop(0, 16, piece, 0)

    def finish_hidden():
        recv_hidden(4, 3, -3, 2, -2, 1, -1, 0)
        keep.wait()
        unpack()

    steps = dict(hid=send_hidden, qx1=qx1, qx2=qx2, qx_end=qx_end, qy=lambda hop: qy(hop) if hop > 1 else qy1(), qy_end=qy_end,
                 gy=lambda hop, p: gy(hop, p) if hop > 1 else gy1(p), gy_end=gy_end, gx1=gx1, gx2=gx2, gx_end=gx_end,
                 dks=dk_send, dz1=dz1, dz=dz, dz_end=dz_end, fin=finish_hidden)
    early, mail.sent = mail.sent, []
    steps["drain"] = lambda: mail.drain(like, kdev, early)
    parts2 = split(backward_order, [(u, r) for r in range(8) for u in ("T", "P")])

    def backward_round(r, _):
        for work, offset in ((terms, 0), (partial, 1)):
            for i in range(8):
                if parts2[2 * i + offset]:
                    pl.when(r == i)(functools.partial(run, steps, parts2[2 * i + offset]))
            work(r)
        return 0

    lax.fori_loop(0, 8, backward_round, 0)
    run(steps, parts2[16])
    mail.drain(like, kdev, mail.sent)


def fused(slots, count, w, tokens, cot):
    vm = pl.BlockSpec(memory_space=pltpu.VMEM)
    hbm = pl.BlockSpec(memory_space=pltpu.HBM)
    V = pltpu.VMEM
    n = 256
    brows = 512 - acut
    return pl.pallas_call(
        kernel_body, name="block_sparse_ffn",
        out_shape=(
            jax.ShapeDtypeStruct((12, 24576), bf16),
            jax.ShapeDtypeStruct((192, 512), bf16),
            jax.ShapeDtypeStruct((512, 128), bf16),
        ),
        in_specs=[hbm] * 5, out_specs=(vm, vm, vm),
        scratch_shapes=[
            V((8, 4, wrows, 128), bf16), V((8, 2, 192, 512), bf16), V((192, 1536), f32),
            V((8, 4, 8, 128), jnp.int32), pltpu.SMEM((8, 4, 8, 128), jnp.int32),
            V((17, 128, 128), bf16), V((192, 1536), f32), V((12, 192, 128), bf16), V((192, 128), f32),
            V((16, 16, 1152), f32), V((16, 16, 1152), bf16), V((16, 16, 1152), bf16),
            V((8, 4, 512, 128), bf16), V((8, 2, 192, 512), bf16),
            V((2, 4, 4, acut, 128), bf16), V((2, 2, acut, 128), bf16),
            V((2, 2, 8, brows, 128), bf16), V((2, 4, brows, 128), bf16),
            V((8, 192, 512), bf16), V((2, 4, 192, 512), bf16),
            pltpu.SMEM((4,), jnp.int32), pltpu.SMEM((1,), jnp.int32),
            pltpu.SemaphoreType.DMA((n,)), pltpu.SemaphoreType.DMA((n,)),
            pltpu.SemaphoreType.DMA((6,)), pltpu.SemaphoreType.DMA((8,)),
        ],
        compiler_params=pltpu.CompilerParams(collective_id=0, has_side_effects=True, vmem_limit_bytes=48 * 2**20),
    )(slots, count, w, tokens, cot)


def place_body(*refs):
    n = len(refs) // 2
    copies = [pltpu.make_async_copy(refs[i], refs[n + i], refs[-1].at[i]) for i in range(n)]
    for c in copies:
        c.start()
    for c in copies:
        c.wait()


def place(*arrays):
    return pl.pallas_call(
        place_body, name="place",
        out_shape=[jax.ShapeDtypeStruct(a.shape, a.dtype) for a in arrays],
        in_specs=[pl.BlockSpec(memory_space=pltpu.VMEM)] * len(arrays),
        out_specs=[pl.BlockSpec(memory_space=pltpu.HBM)] * len(arrays),
        scratch_shapes=[pltpu.SemaphoreType.DMA((len(arrays),))],
        compiler_params=pltpu.CompilerParams(vmem_limit_bytes=8 * 2**20),
    )(*arrays)


def body(tokens, weight_blocks, block_slots, block_counts, cotangent):
    hidden, dx, dw = fused(
        pltpu.with_memory_space_constraint(block_slots.reshape(4), pltpu.HBM), block_counts.reshape(1),
        *(pltpu.with_memory_space_constraint(a, pltpu.HBM) for a in (weight_blocks.reshape(512, 128), tokens, cotangent))
    )
    hidden, dx, dw = place(hidden, dx, dw)
    return hidden, dx, dw.reshape(1, 1, 4, 128, 128)


def solution(mesh):
    in_specs = (
        P("row", "col"),
        P("row", "col", None, None, None),
        P("row", "col", None),
        P("row", "col"),
        P("row", "col"),
    )
    out_specs = (P(("row", "col"), None), P("row", "col"), P("row", "col", None, None, None))
    return jax.shard_map(body, mesh=mesh, in_specs=in_specs, out_specs=out_specs, check_vma=False)
```
